128 devices in a mesh: loop: 8 (over z_hi, y), chan: 16 (over x, z_lo, core).
Axes of the slice: x: 4, y: 4, z: 4 (z_hi: 2, z_lo: 2; z = z_hi * 2 + z_lo), core: 2. Of those that a mesh axis runs over, the one named last changes fastest.
Arguments:
- records: bfloat16 [256, 32768], P('loop', 'chan'), may hold values from -64 to 64
- dead_flags: int32 [256], P('loop'), may hold values 0 or 1
- starts: int32 [32], replicated, may hold values from 0 to 28672, as said below
- offsets: int32 [4], replicated, may hold values from 0 to 128, as said below
Outputs:
- cross_stack: float32 [256, 4, 4096], P(('loop', 'chan'))
The draws below stay inside these ranges and needn't reach their ends.
Inputs may be any that keep to these rules, and one draw needn't show every extreme that they name: `starts`: rising; the first is 0 and the last 28672. `offsets`: the first is 0 and the last 128.
All inputs are finite; a program needn't handle non-finite values. No bound on the sum of `dead_flags` on one device may be relied on, other than what follows from the above.
Results may differ from the reference program's by a relative error of at most 0.0045.
Values may be sent and summed in bfloat16 or wider, within the bound.
No kernel may reach another device: no remote copies, remote signals or barrier semaphores. Data moves between devices by JAX's collectives and lax.ppermute only.
A program may use at most 192 MiB of HBM per device.

```python
import jax
import jax.numpy as jnp
from jax import lax

NT = 32768
NF = 2048
NWIN = 32
NOFF = 4
RMW = 256
WB = 128
WIN = 4096
CH = 256


def draw_records(key, part):
    key = jax.random.fold_in(key, 11)
    subkeys = jax.random.split(key, 5)
    noise_field = jnp.clip(jax.random.normal(subkeys[0], (CH, NT + 3)), -4.0, 4.0)
    common_weight = 0.6
    low_scale = 0.3
    high_scale = 3.0
    filter_taps = jax.random.uniform(subkeys[1], (CH, 3), minval=-0.9, maxval=0.9)
    colored = noise_field[:, 3:] + filter_taps[:, 0:1] * noise_field[:, 2:-1]
    colored = colored + filter_taps[:, 1:2] * noise_field[:, 1:-2] + filter_taps[:, 2:3] * noise_field[:, :-3]
    common = jnp.clip(jax.random.normal(subkeys[2], (NT + 3 * CH,)), -4.0, 4.0)
    lag_index = jnp.arange(NT, dtype=jnp.int32)[None, :] + 3 * jnp.arange(CH, dtype=jnp.int32)[:, None]
    wave_field = jnp.take(common, lag_index)
    chan_scale = jnp.exp(jax.random.uniform(subkeys[3], (CH, 1), minval=jnp.log(low_scale), maxval=jnp.log(high_scale)))
    block_scale = jnp.exp(jax.random.uniform(subkeys[4], (NT // 32,), minval=jnp.log(0.1), maxval=jnp.log(10.0)))
    time_scale = jnp.repeat(block_scale, 32)[None, :]
    result = chan_scale * time_scale * (colored + common_weight * wave_field)
    return jnp.clip(result, -64.0, 64.0).astype(jnp.bfloat16)


def draw_starts(key, part):
    key = jax.random.fold_in(key, 23)
    stride = (NT - WIN) // (NWIN - 1)
    jitter = jax.random.randint(key, (NWIN,), 0, stride // 2 + 1)
    places = jnp.arange(NWIN, dtype=jnp.int32)
    base_start = places * stride + jitter
    chosen = jnp.where(places == 0, 0, jnp.where(places == NWIN - 1, NT - WIN, base_start))
    return chosen.astype(jnp.int32)


def draw_offsets(key, part):
    key = jax.random.fold_in(key, 37)
    middle = jax.random.randint(key, (NOFF,), 1, CH // 2)
    places = jnp.arange(NOFF, dtype=jnp.int32)
    chosen = jnp.where(places == 0, 0, jnp.where(places == NOFF - 1, CH // 2, middle))
    return chosen.astype(jnp.int32)


def set_ends(array, rng, least, high):
    place = [jax.random.randint(jax.random.fold_in(rng, axis), (), 0, length) for axis, length in enumerate(array.shape)]
    longest = array.shape.index(max(array.shape))
    neighbour = place[:longest] + [(place[longest] + 1) % array.shape[longest]] + place[longest + 1:]
    return array.at[tuple(place)].set(least).at[tuple(neighbour)].set(high)


def setup_inputs(seed: int = 0) -> dict:
    seeds = jax.random.split(jax.random.key(seed), 5)
    records = draw_records(jax.random.fold_in(seeds[4], 71), 0)
    dead_flags = set_ends((jax.random.randint(seeds[1], (CH,), 0, 8) < 1).astype(jnp.int32), jax.random.fold_in(seeds[1], 1), 0, 1)
    starts = draw_starts(jax.random.fold_in(seeds[4], 71), 0)
    offsets = draw_offsets(jax.random.fold_in(seeds[4], 71), 0)
    return {"records": records, "dead_flags": dead_flags, "starts": starts, "offsets": offsets}


epsilon = 1e-06

def box_valid(padded, box_width):
    running = padded
    distance = 1
    while distance < box_width:
        running = running[..., :-distance] + running[..., distance:]
        distance *= 2
    return running[..., :padded.shape[-1] - box_width]

def box_sum(values, box_width):
    half_width = box_width // 2
    pad_spec = [(0, 0)] * (values.ndim - 1) + [(half_width, box_width - half_width)]
    return box_valid(jnp.pad(values, pad_spec), box_width)

def box_count(places, box_width, limit):
    upper = jnp.minimum(places + box_width // 2, limit)
    lower = jnp.maximum(places - box_width // 2, 0)
    return (upper - lower).astype(jnp.float32)

def reference(records, dead_flags, starts, offsets):
    live = (1 - dead_flags).astype(jnp.float32)
    signal = records.astype(jnp.float32) * live[:, None]
    sample_index = jnp.arange(NT, dtype=jnp.int32)
    mean_level = box_sum(jnp.abs(signal), RMW) / box_count(sample_index, RMW, NT)[None, :]
    normed = (signal / (mean_level + epsilon)).astype(jnp.bfloat16)
    normed = lax.optimization_barrier(normed)
    bin_index = jnp.arange(NF, dtype=jnp.int32)
    bin_count = box_count(bin_index, WB, NF)
    channel_index = jnp.arange(CH, dtype=jnp.int32)
    partner = ((channel_index[:, None] + offsets[None, :]) % CH).astype(jnp.int32)

    def one_window(running, window_start):
        samples = lax.dynamic_slice_in_dim(normed, window_start, WIN, axis=1).astype(jnp.float32)
        spectrum = jnp.fft.rfft(samples, axis=1)[:, :NF]
        real_part = jnp.real(spectrum)
        imag_part = jnp.imag(spectrum)
        spectral_power = real_part * real_part + imag_part * imag_part
        smooth = box_sum(spectral_power, WB) / bin_count[None, :]
        white_scale = 1.0 / jnp.sqrt(smooth + epsilon)
        white = jnp.concatenate([real_part * white_scale, imag_part * white_scale], axis=1).astype(jnp.bfloat16)
        white = lax.optimization_barrier(white).astype(jnp.float32)
        own_real = white[:, None, :NF]
        own_imag = white[:, None, NF:]
        far_rows = jnp.take(white, partner, axis=0)
        far_real = far_rows[..., :NF]
        far_imag = far_rows[..., NF:]
        cross_real = own_real * far_real + own_imag * far_imag
        cross_imag = own_imag * far_real - own_real * far_imag
        return (running + jnp.concatenate([cross_real, cross_imag], axis=-1), None)
    initial = jnp.zeros((CH, NOFF, 2 * NF), jnp.float32)
    running, _ = lax.scan(one_window, initial, starts)
    return running / NWIN
```

```python
import functools
import math

import jax
import jax.numpy as jnp
import ml_dtypes
import numpy as np
from jax import lax
from jax.experimental import pallas as pl
from jax.experimental.pallas import tpu as pltpu
from jax.sharding import PartitionSpec as P

NT = 32768
NF = 2048
NWIN = 32
NOFF = 4
RMW = 256
WB = 128
WIN = 4096
LANES = 128
PHASES = 16
ROWS = 8
SEGS = ROWS * NWIN
GROUPS = NF // 256

epsilon = 1e-06


def split_table(table):
    high = table.astype(ml_dtypes.bfloat16)
    low = (table - high.astype(np.float64)).astype(ml_dtypes.bfloat16)
    return high, low


@functools.lru_cache(maxsize=None)
def tables():
    n2 = np.arange(256)[:, None]
    f2 = np.arange(LANES)[None, :]
    angle = 2.0 * math.pi * ((n2 * f2) % 256) / 256.0
    first = np.concatenate([np.cos(angle), -np.sin(angle)], axis=1)
    first_high, first_low = split_table(first)

    n1 = np.arange(PHASES)[:, None]
    angle = 2.0 * math.pi * ((n1 * f2) % WIN) / WIN
    twiddle = np.stack([np.cos(angle), np.sin(angle)], axis=1)
    twiddle = np.broadcast_to(twiddle[:, :, None, :], (PHASES, 2, ROWS, LANES))
    twiddle = np.ascontiguousarray(twiddle.reshape(2 * PHASES, ROWS, LANES)).astype(np.float32)

    sample = (np.arange(PHASES)[:, None] + PHASES * np.arange(256)[None, :])[:, :, None]
    group = np.arange(GROUPS)[None, None, :]
    angle = 2.0 * math.pi * (((1 + 2 * group) * sample) % 32) / 32.0
    middle = np.concatenate([np.cos(angle), np.sin(angle)], axis=2)
    high, low = split_table(middle)
    middle = np.zeros((PHASES, 256, LANES), ml_dtypes.bfloat16)
    middle[:, :, :16] = high
    middle[:, :, 16:32] = low

    lane = np.arange(LANES)
    upper = np.where(lane == 0, 128, 256 - lane)
    rows = np.concatenate([upper - 256, lane, upper, lane + 256])[:, None]
    columns = np.concatenate([lane, upper])[None, :]
    box = ((rows >= columns - WB // 2) & (rows < columns + WB // 2)).astype(ml_dtypes.bfloat16)

    bins = np.arange(GROUPS)[:, None] * 256 + np.concatenate([lane, upper])[None, :]
    count = np.minimum(bins + WB // 2, NF) - np.maximum(bins - WB // 2, 0)
    inverse = (1.0 / count).astype(np.float32).reshape(2 * GROUPS, 1, LANES)
    inverse = np.ascontiguousarray(np.broadcast_to(inverse, (2 * GROUPS, ROWS, LANES)))

    flip = np.zeros((LANES, LANES), np.float32)
    flip[(LANES - lane) % LANES, lane] = 1.0
    return first_high, first_low, twiddle, middle, box, inverse, flip


@functools.lru_cache(maxsize=None)
def deal_table():
    column = np.arange(256)
    table = np.zeros((256, 256), ml_dtypes.bfloat16)
    table[(column % 16) * 16 + column // 16, column] = 1.0
    return table


def lane_index(rows=ROWS):
    return lax.broadcasted_iota(jnp.int32, (rows, LANES), 1)


def roll_lanes(value, by):
    return pltpu.roll(value, by % LANES, 1)


def deal_kernel(records_ref, dead_ref, table_ref, out_ref, staged):
    rows = records_ref.shape[0]
    live = (1 - dead_ref[...]).astype(jnp.float32)
    lane = lane_index(rows)
    parts = [[None] * 8, [None] * 8]
    for chunk in range(8):
        product = jnp.dot(
            records_ref[:, chunk * 256 : (chunk + 1) * 256],
            table_ref[...],
            preferred_element_type=jnp.float32,
        )
        parts[0][chunk] = product[:, :LANES]
        parts[1][chunk] = product[:, LANES:]
    for half in range(2):
        current = parts[half]
        for bit in (1, 2, 4):
            step = 16 * bit
            keep = (lane // step) % 2 == 0
            following = list(current)
            for index in range(8):
                if index & bit == 0:
                    low, high = current[index], current[index | bit]
                    following[index] = jnp.where(keep, low, roll_lanes(high, step))
                    following[index | bit] = jnp.where(keep, roll_lanes(low, -step), high)
            current = following
        for index in range(8):
            staged[pl.ds(half * 8 + index, rows, stride=PHASES), :] = current[index] * live
    out_ref[...] = staged[...].reshape(rows, PHASES, LANES).astype(jnp.bfloat16)


def deal(records, dead_flags):
    rows = records.shape[0]
    vmem = pl.BlockSpec(memory_space=pltpu.VMEM)
    return pl.pallas_call(
        deal_kernel,
        out_shape=jax.ShapeDtypeStruct((rows, PHASES, LANES), jnp.bfloat16),
        in_specs=[vmem] * 3,
        out_specs=vmem,
        scratch_shapes=[pltpu.VMEM((rows * PHASES, LANES), jnp.float32)],
        compiler_params=pltpu.CompilerParams(vmem_limit_bytes=16 * 1024 * 1024),
    )(records, dead_flags.reshape(rows, 1), jnp.asarray(deal_table()))


def dft4(a, b, c, d):
    (ar, ai), (br, bi), (cr, ci), (dr, di) = a, b, c, d
    sr, si, tr, ti = ar + cr, ai + ci, ar - cr, ai - ci
    ur, ui, vr, vi = br + dr, bi + di, br - dr, bi - di
    return [(sr + ur, si + ui), (tr + vi, ti - vr), (sr - ur, si - ui), (tr - vi, ti + vr)]


def rotate(value, power):
    re, im = value
    power %= 16
    if power == 0:
        return value
    if power == 4:
        return (im, -re)
    root = math.sqrt(0.5)
    if power == 2:
        return ((re + im) * root, (im - re) * root)
    if power == 6:
        return ((im - re) * root, (re + im) * (-root))
    cos, sin = math.cos(2 * math.pi * power / 16), math.sin(2 * math.pi * power / 16)
    return (re * cos + im * sin, im * cos - re * sin)


def dft16(values):
    inner = [dft4(values[q], values[q + 4], values[q + 8], values[q + 12]) for q in range(4)]
    result = [None] * 16
    for k in range(4):
        outer = dft4(*[rotate(inner[q][k], q * k) for q in range(4)])
        for j in range(4):
            result[k + 4 * j] = outer[j]
    return result


def stack_kernel(
    starts_ref,
    parts_ref,
    high_ref,
    low_ref,
    twiddle_ref,
    middle_ref,
    box_ref,
    inverse_ref,
    flip_ref,
    out_ref,
    plain,
    before,
    after,
    normed,
    segments,
    middles,
    spectrum,
    power,
    smooth,
    folded,
):
    lane = lane_index()
    shards = parts_ref.shape[0]
    plain[...] = parts_ref[...].reshape(shards, ROWS * PHASES, LANES).astype(jnp.float32)

    totals = []
    for k in range(shards):
        level = [
            jnp.abs(plain[k, pl.ds(p, ROWS, stride=PHASES), :]) for p in range(PHASES)
        ]
        running = jnp.zeros((ROWS, LANES), jnp.float32)
        for p in range(PHASES):
            before[p, k] = running
            running = running + level[p]
        totals.append(running)
        running = jnp.zeros((ROWS, LANES), jnp.float32)
        for p in reversed(range(PHASES)):
            running = running + level[p]
            after[p, k] = running
    zero = jnp.zeros((ROWS, LANES), jnp.float32)

    def ahead(tiles, by):
        rolled = [roll_lanes(tile, -by) for tile in tiles] + [zero]
        return [jnp.where(lane < LANES - by, rolled[k], rolled[k + 1]) for k in range(len(tiles))]

    def behind(tiles, by):
        rolled = [zero] + [roll_lanes(tile, by) for tile in tiles]
        return [jnp.where(lane >= by, rolled[k + 1], rolled[k]) for k in range(len(tiles))]

    def plus(*lists):
        return [functools.reduce(lambda a, b: a + b, group) for group in zip(*lists)]

    two = plus(totals, ahead(totals, 1))
    four = plus(two, ahead(two, 2))
    columns = plus(ahead(four, 1), ahead(two, 5), ahead(totals, 7))
    past = totals
    for by in (1, 2, 4):
        past = plus(past, behind(past, by))
    columns = plus(columns, past)
    for k in range(shards):
        smooth[pl.ds(k * ROWS, ROWS), pl.ds(0, LANES)] = columns[k]

    def normalize(p, carry):
        first = behind([after[p, k] for k in range(shards)], 8)
        last = ahead([before[p, k] for k in range(shards)], 8)
        for k in range(shards):
            full = smooth[pl.ds(k * ROWS, ROWS), pl.ds(0, LANES)]
            total = full + first[k] + last[k]
            if k in (0, shards - 1):
                place = p + PHASES * (k * LANES + lane)
                count = jnp.minimum(place + RMW // 2, NT) - jnp.maximum(place - RMW // 2, 0)
                mean_level = total / count.astype(jnp.float32)
            else:
                mean_level = total * (1.0 / RMW)
            signal = plain[k, pl.ds(p, ROWS, stride=PHASES), :]
            ratio = signal / (mean_level + epsilon)
            normed[p, k] = ratio.astype(jnp.bfloat16).astype(jnp.float32)
        normed[p, shards] = zero
        return carry

    lax.fori_loop(0, PHASES, normalize, 0)

    def cut(w, carry):
        start = starts_ref[w]
        phase = start & (PHASES - 1)
        column = start >> 4
        for n1 in range(PHASES):
            place = phase + n1
            here = column + (place >> 4)
            tile = here >> 7
            by = here & (LANES - 1)
            p = place & (PHASES - 1)
            a, b, c = normed[p, tile], normed[p, tile + 1], normed[p, tile + 2]
            keep = lane >= by
            turn = (LANES - by) & (LANES - 1)
            segments[2 * n1, pl.ds(w, ROWS, stride=NWIN), :] = pltpu.roll(
                jnp.where(keep, a, b), turn, 1
            )
            segments[2 * n1 + 1, pl.ds(w, ROWS, stride=NWIN), :] = pltpu.roll(
                jnp.where(keep, b, c), turn, 1
            )
        return carry

    lax.fori_loop(0, NWIN, cut, 0)

    middles[...] = jnp.zeros_like(middles)

    def transform(n1, carry):
        left = jnp.concatenate([segments[2 * n1], segments[2 * n1 + 1]], axis=1)
        left = left.astype(jnp.bfloat16)
        product = jnp.dot(left, high_ref[...], preferred_element_type=jnp.float32)
        product = product + jnp.dot(left, low_ref[...], preferred_element_type=jnp.float32)
        middles[...] += jnp.dot(left, middle_ref[n1], preferred_element_type=jnp.float32)
        segments[2 * n1] = product[:, :LANES]
        segments[2 * n1 + 1] = product[:, LANES:]
        return carry

    lax.fori_loop(0, PHASES, transform, 0)

    zero_pair = jnp.zeros((SEGS, LANES), jnp.bfloat16)
    power[:, pl.ds(0, LANES)] = zero_pair
    power[:, pl.ds((2 * GROUPS + 1) * LANES, LANES)] = zero_pair

    def combine(pair, carry):
        powers = []
        for part in range(2):
            rows = pl.ds(pl.multiple_of(pair * 16 + part * ROWS, ROWS), ROWS)
            values = []
            for n1 in range(PHASES):
                re, im = segments[2 * n1, rows, :], segments[2 * n1 + 1, rows, :]
                if n1:
                    cos, sin = twiddle_ref[2 * n1], twiddle_ref[2 * n1 + 1]
                    re, im = re * cos + im * sin, im * cos - re * sin
                values.append((re, im))
            values = dft16(values)
            centre = middles[rows, :]
            centre = centre + roll_lanes(centre, -16)
            squares = []
            for g in range(GROUPS):
                for side in range(2):
                    re, im = values[15 - g] if side else values[g]
                    if side:
                        re = jnp.where(lane == 0, roll_lanes(centre, -g), re)
                        im = jnp.where(lane == 0, roll_lanes(centre, -(GROUPS + g)), im)
                    spectrum[4 * g + 2 * side, rows, :] = re
                    spectrum[4 * g + 2 * side + 1, rows, :] = im
                    squares.append(re * re + im * im)
            powers.append(squares)
        both = pl.ds(pl.multiple_of(pair * 16, 16), 16)
        for tile in range(2 * GROUPS):
            joined = jnp.concatenate([powers[0][tile], powers[1][tile]], axis=0)
            power[both, pl.ds((tile + 1) * LANES, LANES)] = joined.astype(jnp.bfloat16)
        return carry

    lax.fori_loop(0, SEGS // 16, combine, 0)

    for g in range(GROUPS):
        smooth[...] = jnp.dot(
            power[:, g * 256 : g * 256 + 512], box_ref[...], preferred_element_type=jnp.float32
        )
        for side in range(2):
            inverse = inverse_ref[2 * g + side]
            for c in range(2):
                sums = None
                for octet in range(NWIN // 8):
                    white = []
                    for o in range(NOFF):
                        rows = pl.ds((2 * o + c) * NWIN + octet * 8, 8)
                        level = smooth[rows, side * LANES : (side + 1) * LANES] * inverse
                        scale = lax.rsqrt(level + epsilon)
                        re = spectrum[4 * g + 2 * side, rows, :] * scale
                        im = spectrum[4 * g + 2 * side + 1, rows, :] * scale
                        white.append((re, im))
                    own_re, own_im = white[0]
                    terms = [own_re * own_re + own_im * own_im]
                    for far_re, far_im in white[1:]:
                        terms.append(own_re * far_re + own_im * far_im)
                        if side:
                            terms.append(own_re * far_im - own_im * far_re)
                        else:
                            terms.append(own_im * far_re - own_re * far_im)
                    sums = terms if sums is None else [a + b for a, b in zip(sums, terms)]
                sums = [jnp.sum(x, axis=0, keepdims=True) * (1.0 / NWIN) for x in sums]
                real = jnp.concatenate([sums[0], sums[1], sums[3], sums[5]], axis=0)
                nothing = jnp.zeros((1, LANES), jnp.float32)
                imag = jnp.concatenate([nothing, sums[2], sums[4], sums[6]], axis=0)
                if side:
                    folded[pl.ds((g * 2 + c) * 8, 4), :] = real
                    folded[pl.ds((g * 2 + c) * 8 + 4, 4), :] = imag
                else:
                    out_ref[c, :, pl.ds(g * 256, LANES)] = real
                    out_ref[c, :, pl.ds(NF + g * 256, LANES)] = imag
    folded[...] = jnp.dot(
        folded[...],
        flip_ref[...],
        preferred_element_type=jnp.float32,
        precision=lax.Precision.HIGHEST,
    )
    for g in range(GROUPS):
        for c in range(2):
            row = (g * 2 + c) * 8
            out_ref[c, :, pl.ds(g * 256 + LANES, LANES)] = folded[pl.ds(row, 4), :]
            out_ref[c, :, pl.ds(NF + g * 256 + LANES, LANES)] = folded[pl.ds(row + 4, 4), :]


def stack(parts, starts):
    shards = parts.shape[0]
    vmem = pl.BlockSpec(memory_space=pltpu.VMEM)
    f32 = jnp.float32
    return pl.pallas_call(
        stack_kernel,
        out_shape=jax.ShapeDtypeStruct((2, NOFF, 2 * NF), f32),
        in_specs=[pl.BlockSpec(memory_space=pltpu.SMEM)] + [vmem] * 8,
        out_specs=vmem,
        scratch_shapes=[
            pltpu.VMEM((shards, ROWS * PHASES, LANES), f32),
            pltpu.VMEM((PHASES, shards, ROWS, LANES), f32),
            pltpu.VMEM((PHASES, shards, ROWS, LANES), f32),
            pltpu.VMEM((PHASES, shards + 1, ROWS, LANES), f32),
            pltpu.VMEM((2 * PHASES, SEGS, LANES), f32),
            pltpu.VMEM((SEGS, LANES), f32),
            pltpu.VMEM((4 * GROUPS, SEGS, LANES), f32),
            pltpu.VMEM((SEGS, (2 * GROUPS + 2) * LANES), jnp.bfloat16),
            pltpu.VMEM((SEGS, 2 * LANES), f32),
            pltpu.VMEM((2 * GROUPS * 8, LANES), f32),
        ],
        compiler_params=pltpu.CompilerParams(vmem_limit_bytes=40 * 1024 * 1024),
    )(starts, parts, *[jnp.asarray(table) for table in tables()])


def ahead_on(array, axis, by):
    size = lax.axis_size(axis)
    return lax.ppermute(array, axis, [((i + by) % size, i) for i in range(size)])


def body(records, dead_flags, starts, offsets):
    rows = records.shape[0]
    dealt = deal(records, dead_flags)
    reach = lax.axis_size("loop") // 2
    blocks = [dealt] + [ahead_on(dealt, "loop", by) for by in range(1, reach + 1)]
    nearby = jnp.concatenate(blocks, axis=0)
    members = lax.axis_size("chan")
    picked = [
        lax.dynamic_slice_in_dim(nearby, offsets[o], rows, 0).reshape(
            members, rows // members, PHASES, LANES
        )
        for o in range(NOFF)
    ]
    outgoing = jnp.concatenate(picked, axis=1)
    parts = lax.all_to_all(outgoing, "chan", split_axis=0, concat_axis=0, tiled=True)
    return stack(parts, starts)


def solution(mesh):
    in_specs = (P("loop", "chan"), P("loop"), P(), P())
    out_specs = P(("loop", "chan"), None, None)
    return jax.shard_map(body, mesh=mesh, in_specs=in_specs, out_specs=out_specs, check_vma=False)
```

```python
import functools
import math

import jax
import jax.numpy as jnp
import ml_dtypes
import numpy as np
from jax import lax
from jax.experimental import pallas as pl
from jax.experimental.pallas import tpu as pltpu
from jax.sharding import PartitionSpec as P

NT = 32768
NF = 2048
NWIN = 32
NOFF = 4
RMW = 256
WB = 128
WIN = 4096
LANES = 128
PHASES = 16
PITCH = PHASES + 1
ROWS = 8
SEGS = ROWS * NWIN
GROUPS = NF // 256

epsilon = 1e-06


def split_table(table):
    high = table.astype(ml_dtypes.bfloat16)
    low = (table - high.astype(np.float64)).astype(ml_dtypes.bfloat16)
    return high, low


@functools.lru_cache(maxsize=None)
def tables():
    n2 = np.arange(256)[:, None]
    f2 = np.arange(LANES)[None, :]
    angle = 2.0 * math.pi * ((n2 * f2) % 256) / 256.0
    first = np.concatenate([np.cos(angle), -np.sin(angle)], axis=1)
    first_high, first_low = split_table(first)

    n1 = np.arange(PHASES)[:, None]
    angle = 2.0 * math.pi * ((n1 * f2) % WIN) / WIN
    twiddle = np.stack([np.cos(angle), np.sin(angle)], axis=1)
    twiddle = np.broadcast_to(twiddle[:, :, None, :], (PHASES, 2, ROWS, LANES))
    twiddle = np.ascontiguousarray(twiddle.reshape(2 * PHASES, ROWS, LANES)).astype(np.float32)

    sample = (np.arange(PHASES)[:, None] + PHASES * np.arange(256)[None, :])[:, :, None]
    group = np.arange(GROUPS)[None, None, :]
    angle = 2.0 * math.pi * (((1 + 2 * group) * sample) % 32) / 32.0
    middle = np.concatenate([np.cos(angle), np.sin(angle)], axis=2)
    high, low = split_table(middle)
    middle = np.zeros((PHASES, 256, LANES), ml_dtypes.bfloat16)
    middle[:, :, :16] = high
    middle[:, :, 16:32] = low

    lane = np.arange(LANES)
    upper = np.where(lane == 0, 128, 256 - lane)
    rows = np.concatenate([upper - 256, lane, upper, lane + 256])[:, None]
    columns = np.concatenate([lane, upper])[None, :]
    box = ((rows >= columns - WB // 2) & (rows < columns + WB // 2)).astype(ml_dtypes.bfloat16)

    bins = np.arange(GROUPS)[:, None] * 256 + np.concatenate([lane, upper])[None, :]
    count = np.minimum(bins + WB // 2, NF) - np.maximum(bins - WB // 2, 0)
    inverse = (1.0 / count).astype(np.float32).reshape(2 * GROUPS, 1, LANES)
    inverse = np.ascontiguousarray(np.broadcast_to(inverse, (2 * GROUPS, ROWS, LANES)))

    flip = np.zeros((LANES, LANES), np.float32)
    flip[(LANES - lane) % LANES, lane] = 1.0
    return first_high, first_low, twiddle, middle, box, inverse, flip


def lane_index(rows=ROWS):
    return lax.broadcasted_iota(jnp.int32, (rows, LANES), 1)


def roll_lanes(value, by):
    return pltpu.roll(value, by % LANES, 1)


def deal_kernel(records_ref, dead_ref, out_ref, staged):
    rows = records_ref.shape[0]
    place = lax.broadcasted_iota(jnp.int32, (rows, rows), 0)
    across = lax.broadcasted_iota(jnp.int32, (rows, rows), 1)
    live = (1 - dead_ref[...]).astype(jnp.float32)
    live = jnp.sum(jnp.where(place == across, live, 0.0), axis=1, keepdims=True)
    source = lax.broadcasted_iota(jnp.int32, (256, 256), 0)
    target = lax.broadcasted_iota(jnp.int32, (256, 256), 1)
    table = (source == (target % 16) * 16 + target // 16).astype(jnp.bfloat16)
    lane = lane_index(rows)
    parts = [[None] * 8, [None] * 8]
    for chunk in range(8):
        product = jnp.dot(
            records_ref[:, chunk * 256 : (chunk + 1) * 256],
            table,
            preferred_element_type=jnp.float32,
        )
        parts[0][chunk] = product[:, :LANES]
        parts[1][chunk] = product[:, LANES:]
    for half in range(2):
        current = parts[half]
        for bit in (1, 2, 4):
            step = 16 * bit
            keep = (lane // step) % 2 == 0
            following = list(current)
            for index in range(8):
                if index & bit == 0:
                    low, high = current[index], current[index | bit]
                    following[index] = jnp.where(keep, low, roll_lanes(high, step))
                    following[index | bit] = jnp.where(keep, roll_lanes(low, -step), high)
            current = following
        for index in range(8):
            staged[pl.ds(half * 8 + index, rows, stride=PITCH), :] = current[index] * live
    for r in range(rows):
        out_ref[r] = staged[pl.ds(r * PITCH, PHASES), :].astype(jnp.bfloat16)


def deal(records, dead_flags):
    rows = records.shape[0]
    vmem = pl.BlockSpec(memory_space=pltpu.VMEM)
    return pl.pallas_call(
        deal_kernel,
        out_shape=jax.ShapeDtypeStruct((rows, PHASES, LANES), jnp.bfloat16),
        in_specs=[vmem] * 2,
        out_specs=vmem,
        scratch_shapes=[pltpu.VMEM((rows * PITCH, LANES), jnp.float32)],
        compiler_params=pltpu.CompilerParams(vmem_limit_bytes=16 * 1024 * 1024),
    )(records, dead_flags.reshape(1, rows))


def dft4(a, b, c, d):
    (ar, ai), (br, bi), (cr, ci), (dr, di) = a, b, c, d
    sr, si, tr, ti = ar + cr, ai + ci, ar - cr, ai - ci
    ur, ui, vr, vi = br + dr, bi + di, br - dr, bi - di
    return [(sr + ur, si + ui), (tr + vi, ti - vr), (sr - ur, si - ui), (tr - vi, ti + vr)]


def rotate(value, power):
    re, im = value
    power %= 16
    if power == 0:
        return value
    if power == 4:
        return (im, -re)
    root = math.sqrt(0.5)
    if power == 2:
        return ((re + im) * root, (im - re) * root)
    if power == 6:
        return ((im - re) * root, (re + im) * (-root))
    cos, sin = math.cos(2 * math.pi * power / 16), math.sin(2 * math.pi * power / 16)
    return (re * cos + im * sin, im * cos - re * sin)


def dft16(values):
    inner = [dft4(values[q], values[q + 4], values[q + 8], values[q + 12]) for q in range(4)]
    result = [None] * 16
    for k in range(4):
        outer = dft4(*[rotate(inner[q][k], q * k) for q in range(4)])
        for j in range(4):
            result[k + 4 * j] = outer[j]
    return result


def stack_kernel(
    starts_ref,
    parts_ref,
    high_ref,
    low_ref,
    twiddle_ref,
    middle_ref,
    box_ref,
    inverse_ref,
    flip_ref,
    out_ref,
    plain,
    before,
    after,
    normed,
    segments,
    samples,
    factor,
    middles,
    spectrum,
    power,
    smooth,
    folded,
):
    lane = lane_index()
    shards = parts_ref.shape[0]
    for k in range(shards):
        for r in range(ROWS):
            plain[k, pl.ds(r * PITCH, PHASES), :] = parts_ref[k, r].astype(jnp.float32)

    totals = []
    for k in range(shards):
        level = [
            jnp.abs(plain[k, pl.ds(p, ROWS, stride=PITCH), :]) for p in range(PHASES)
        ]
        running = jnp.zeros((ROWS, LANES), jnp.float32)
        for p in range(PHASES):
            before[p, k] = running
            running = running + level[p]
        totals.append(running)
        running = jnp.zeros((ROWS, LANES), jnp.float32)
        for p in reversed(range(PHASES)):
            running = running + level[p]
            after[p, k] = running
    zero = jnp.zeros((ROWS, LANES), jnp.float32)

    def ahead(tiles, by):
        rolled = [roll_lanes(tile, -by) for tile in tiles] + [zero]
        return [jnp.where(lane < LANES - by, rolled[k], rolled[k + 1]) for k in range(len(tiles))]

    def behind(tiles, by):
        rolled = [zero] + [roll_lanes(tile, by) for tile in tiles]
        return [jnp.where(lane >= by, rolled[k + 1], rolled[k]) for k in range(len(tiles))]

    def plus(*lists):
        return [functools.reduce(lambda a, b: a + b, group) for group in zip(*lists)]

    two = plus(totals, ahead(totals, 1))
    four = plus(two, ahead(two, 2))
    columns = plus(ahead(four, 1), ahead(two, 5), ahead(totals, 7))
    past = totals
    for by in (1, 2, 4):
        past = plus(past, behind(past, by))
    columns = plus(columns, past)
    for k in range(shards):
        smooth[pl.ds(k * ROWS, ROWS), pl.ds(0, LANES)] = columns[k]

    def normalize(p, carry):
        first = behind([after[p, k] for k in range(shards)], 8)
        last = ahead([before[p, k] for k in range(shards)], 8)
        tiles = []
        for k in range(shards):
            full = smooth[pl.ds(k * ROWS, ROWS), pl.ds(0, LANES)]
            total = full + first[k] + last[k]
            if k in (0, shards - 1):
                place = p + PHASES * (k * LANES + lane)
                count = jnp.minimum(place + RMW // 2, NT) - jnp.maximum(place - RMW // 2, 0)
                mean_level = total / count.astype(jnp.float32)
            else:
                mean_level = total * (1.0 / RMW)
            signal = plain[k, pl.ds(p, ROWS, stride=PITCH), :]
            ratio = signal / (mean_level + epsilon)
            tiles.append(ratio.astype(jnp.bfloat16).astype(jnp.float32))
        for k, (tile, later) in enumerate(zip(tiles, ahead(tiles, 1))):
            normed[p, k] = tile
            normed[p + PHASES, k] = later
        normed[p, shards] = zero
        normed[p + PHASES, shards] = zero
        return carry

    lax.fori_loop(0, PHASES, normalize, 0, unroll=4)

    def cut(w, carry):
        start = starts_ref[w]
        phase = start & (PHASES - 1)
        column = start >> 4
        tile = column >> 7
        by = column & (LANES - 1)
        keep = lane >= by
        turn = (LANES - by) & (LANES - 1)
        for n1 in range(PHASES):
            a, b, c = [normed[phase + n1, tile + step] for step in range(3)]
            for half, joined in enumerate((jnp.where(keep, a, b), jnp.where(keep, b, c))):
                rows = pl.ds(w, ROWS, stride=NWIN + 1)
                segments[2 * n1 + half, rows, :] = pltpu.roll(joined, turn, 1)
        return carry

    lax.fori_loop(0, NWIN, cut, 0, unroll=4)

    for n1 in range(PHASES):
        for r in range(ROWS):
            both = jnp.concatenate(
                [segments[2 * n1 + h, pl.ds(r * (NWIN + 1), NWIN), :] for h in range(2)], axis=1
            )
            samples[n1, pl.ds(r * NWIN, NWIN), :] = both.astype(jnp.bfloat16)
    left = samples[...].reshape(PHASES * SEGS, 2 * LANES)
    product = jnp.dot(left, high_ref[...], preferred_element_type=jnp.float32)
    product = product + jnp.dot(left, low_ref[...], preferred_element_type=jnp.float32)
    factor[...] = product.reshape(PHASES, SEGS, 2 * LANES)
    left = jnp.concatenate([samples[n1] for n1 in range(PHASES)], axis=1)
    middles[...] = jnp.dot(
        left, middle_ref[...].reshape(WIN, LANES), preferred_element_type=jnp.float32
    )

    zero_pair = jnp.zeros((SEGS, LANES), jnp.bfloat16)
    power[:, pl.ds(0, LANES)] = zero_pair
    power[:, pl.ds((2 * GROUPS + 1) * LANES, LANES)] = zero_pair

    def combine(pair, carry):
        powers = []
        for part in range(2):
            rows = pl.ds(pl.multiple_of(pair * 16 + part * ROWS, ROWS), ROWS)
            values = []
            for n1 in range(PHASES):
                re, im = factor[n1, rows, pl.ds(0, LANES)], factor[n1, rows, pl.ds(LANES, LANES)]
                if n1:
                    cos, sin = twiddle_ref[2 * n1], twiddle_ref[2 * n1 + 1]
                    re, im = re * cos + im * sin, im * cos - re * sin
                values.append((re, im))
            values = dft16(values)
            centre = middles[rows, :]
            centre = centre + roll_lanes(centre, -16)
            squares = []
            for g in range(GROUPS):
                for side in range(2):
                    re, im = values[15 - g] if side else values[g]
                    if side:
                        re = jnp.where(lane == 0, roll_lanes(centre, -g), re)
                        im = jnp.where(lane == 0, roll_lanes(centre, -(GROUPS + g)), im)
                    spectrum[4 * g + 2 * side, rows, :] = re
                    spectrum[4 * g + 2 * side + 1, rows, :] = im
                    squares.append(re * re + im * im)
            powers.append(squares)
        both = pl.ds(pl.multiple_of(pair * 16, 16), 16)
        for tile in range(2 * GROUPS):
            joined = jnp.concatenate([powers[0][tile], powers[1][tile]], axis=0)
            power[both, pl.ds((tile + 1) * LANES, LANES)] = joined.astype(jnp.bfloat16)
        return carry

    lax.fori_loop(0, SEGS // 16, combine, 0, unroll=4)

    for g in range(GROUPS):
        smooth[...] = jnp.dot(
            power[:, g * 256 : g * 256 + 512], box_ref[...], preferred_element_type=jnp.float32
        )
        for side in range(2):
            inverse = inverse_ref[2 * g + side]
            for c in range(2):
                sums = None
                for octet in range(NWIN // 8):
                    white = []
                    for o in range(NOFF):
                        rows = pl.ds((2 * o + c) * NWIN + octet * 8, 8)
                        level = smooth[rows, side * LANES : (side + 1) * LANES] * inverse
                        scale = lax.rsqrt(level + epsilon)
                        re = spectrum[4 * g + 2 * side, rows, :] * scale
                        im = spectrum[4 * g + 2 * side + 1, rows, :] * scale
                        white.append((re, im))
                    own_re, own_im = white[0]
                    terms = [own_re * own_re + own_im * own_im]
                    for far_re, far_im in white[1:]:
                        terms.append(own_re * far_re + own_im * far_im)
                        if side:
                            terms.append(own_re * far_im - own_im * far_re)
                        else:
                            terms.append(own_im * far_re - own_re * far_im)
                    sums = terms if sums is None else [a + b for a, b in zip(sums, terms)]
                sums = [jnp.sum(x, axis=0, keepdims=True) * (1.0 / NWIN) for x in sums]
                real = jnp.concatenate([sums[0], sums[1], sums[3], sums[5]], axis=0)
                nothing = jnp.zeros((1, LANES), jnp.float32)
                imag = jnp.concatenate([nothing, sums[2], sums[4], sums[6]], axis=0)
                if side:
                    folded[pl.ds((g * 2 + c) * 8, 4), :] = real
                    folded[pl.ds((g * 2 + c) * 8 + 4, 4), :] = imag
                else:
                    out_ref[c, :, pl.ds(g * 256, LANES)] = real
                    out_ref[c, :, pl.ds(NF + g * 256, LANES)] = imag
    folded[...] = jnp.dot(
        folded[...],
        flip_ref[...],
        preferred_element_type=jnp.float32,
        precision=lax.Precision.HIGHEST,
    )
    for g in range(GROUPS):
        for c in range(2):
            row = (g * 2 + c) * 8
            out_ref[c, :, pl.ds(g * 256 + LANES, LANES)] = folded[pl.ds(row, 4), :]
            out_ref[c, :, pl.ds(NF + g * 256 + LANES, LANES)] = folded[pl.ds(row + 4, 4), :]


def stack(parts, starts):
    shards = parts.shape[0]
    vmem = pl.BlockSpec(memory_space=pltpu.VMEM)
    f32 = jnp.float32
    return pl.pallas_call(
        stack_kernel,
        out_shape=jax.ShapeDtypeStruct((2, NOFF, 2 * NF), f32),
        in_specs=[pl.BlockSpec(memory_space=pltpu.SMEM)] + [vmem] * 8,
        out_specs=vmem,
        scratch_shapes=[
            pltpu.VMEM((shards, ROWS * PITCH, LANES), f32),
            pltpu.VMEM((PHASES, shards, ROWS, LANES), f32),
            pltpu.VMEM((PHASES, shards, ROWS, LANES), f32),
            pltpu.VMEM((2 * PHASES, shards + 1, ROWS, LANES), f32),
            pltpu.VMEM((2 * PHASES, ROWS * (NWIN + 1), LANES), f32),
            pltpu.VMEM((PHASES, SEGS, 2 * LANES), jnp.bfloat16),
            pltpu.VMEM((PHASES, SEGS, 2 * LANES), f32),
            pltpu.VMEM((SEGS, LANES), f32),
            pltpu.VMEM((4 * GROUPS, SEGS, LANES), f32),
            pltpu.VMEM((SEGS, (2 * GROUPS + 2) * LANES), jnp.bfloat16),
            pltpu.VMEM((SEGS, 2 * LANES), f32),
            pltpu.VMEM((2 * GROUPS * 8, LANES), f32),
        ],
        compiler_params=pltpu.CompilerParams(vmem_limit_bytes=40 * 1024 * 1024),
    )(starts, parts, *[jnp.asarray(table) for table in tables()])


def ahead_on(array, axis, by):
    size = lax.axis_size(axis)
    return lax.ppermute(array, axis, [((i + by) % size, i) for i in range(size)])


def body(records, dead_flags, starts, offsets):
    rows = records.shape[0]
    dealt = deal(records, dead_flags)
    reach = lax.axis_size("loop") // 2
    blocks = [dealt] + [ahead_on(dealt, "loop", by) for by in range(1, reach + 1)]
    nearby = jnp.concatenate(blocks, axis=0)
    members = lax.axis_size("chan")
    picked = [
        lax.dynamic_slice_in_dim(nearby, offsets[o], rows, 0).reshape(
            members, rows // members, PHASES, LANES
        )
        for o in range(NOFF)
    ]
    outgoing = jnp.concatenate(picked, axis=1)
    parts = lax.all_to_all(outgoing, "chan", split_axis=0, concat_axis=0, tiled=True)
    return stack(parts, starts)


def solution(mesh):
    in_specs = (P("loop", "chan"), P("loop"), P(), P())
    out_specs = P(("loop", "chan"), None, None)
    return jax.shard_map(body, mesh=mesh, in_specs=in_specs, out_specs=out_specs, check_vma=False)
```

```python
import functools
import math

import jax
import jax.numpy as jnp
import ml_dtypes
import numpy as np
from jax import lax
from jax.experimental import pallas as pl
from jax.experimental.pallas import tpu as pltpu
from jax.sharding import PartitionSpec as P

NT = 32768
NF = 2048
NWIN = 32
NOFF = 4
RMW = 256
WB = 128
WIN = 4096
LANES = 128
PHASES = 16
PITCH = PHASES + 1
ROWS = 8
SEGS = ROWS * NWIN
GROUPS = NF // 256

epsilon = 1e-06


def split_table(table):
    high = table.astype(ml_dtypes.bfloat16)
    low = (table - high.astype(np.float64)).astype(ml_dtypes.bfloat16)
    return high, low


@functools.lru_cache(maxsize=None)
def tables():
    n2 = np.arange(256)[:, None]
    f2 = np.arange(LANES)[None, :]
    angle = 2.0 * math.pi * ((n2 * f2) % 256) / 256.0
    first = np.concatenate([np.cos(angle), -np.sin(angle)], axis=1)
    first_high, first_low = split_table(first)

    n1 = np.arange(PHASES)[:, None]
    angle = 2.0 * math.pi * ((n1 * f2) % WIN) / WIN
    twiddle = np.stack([np.cos(angle), np.sin(angle)], axis=1)
    twiddle = np.broadcast_to(twiddle[:, :, None, :], (PHASES, 2, ROWS, LANES))
    twiddle = np.ascontiguousarray(twiddle.reshape(2 * PHASES, ROWS, LANES)).astype(np.float32)

    sample = (np.arange(PHASES)[:, None] + PHASES * np.arange(256)[None, :])[:, :, None]
    group = np.arange(GROUPS)[None, None, :]
    angle = 2.0 * math.pi * (((1 + 2 * group) * sample) % 32) / 32.0
    middle = np.concatenate([np.cos(angle), np.sin(angle)], axis=2)
    high, low = split_table(middle)
    middle = np.zeros((PHASES, 256, LANES), ml_dtypes.bfloat16)
    middle[:, :, :16] = high
    middle[:, :, 16:32] = low

    lane = np.arange(LANES)
    upper = np.where(lane == 0, 128, 256 - lane)
    rows = np.concatenate([upper - 256, lane, upper, lane + 256])[:, None]
    columns = np.concatenate([lane, upper])[None, :]
    box = ((rows >= columns - WB // 2) & (rows < columns + WB // 2)).astype(ml_dtypes.bfloat16)

    bins = np.arange(GROUPS)[:, None] * 256 + np.concatenate([lane, upper])[None, :]
    count = np.minimum(bins + WB // 2, NF) - np.maximum(bins - WB // 2, 0)
    inverse = (1.0 / count).astype(np.float32).reshape(2 * GROUPS, 1, LANES)
    inverse = np.ascontiguousarray(np.broadcast_to(inverse, (2 * GROUPS, ROWS, LANES)))

    flip = np.zeros((LANES, LANES), np.float32)
    flip[(LANES - lane) % LANES, lane] = 1.0
    row = np.arange(2 * LANES)[:, None]
    shift = np.concatenate([row == 120 + lane[None, :], row == 8 + lane[None, :]], axis=1)
    shift = shift.astype(ml_dtypes.bfloat16)
    return shift, first_high, first_low, twiddle, middle, box, inverse, flip


def lane_index(rows=ROWS):
    return lax.broadcasted_iota(jnp.int32, (rows, LANES), 1)


def roll_lanes(value, by):
    return pltpu.roll(value, by % LANES, 1)


def deal_kernel(records_hbm, dead_hbm, out_ref, records_ref, dead_ref, staged, sems):
    rows = records_hbm.shape[0]
    copies = [
        pltpu.make_async_copy(dead_hbm, dead_ref, sems.at[0]),
        pltpu.make_async_copy(records_hbm, records_ref, sems.at[1]),
    ]
    for copy in copies:
        copy.start()
    source = lax.broadcasted_iota(jnp.int32, (256, 256), 0)
    target = lax.broadcasted_iota(jnp.int32, (256, 256), 1)
    table = (source == (target % 16) * 16 + target // 16).astype(jnp.bfloat16)
    copies[0].wait()
    place = lax.broadcasted_iota(jnp.int32, (rows, rows), 0)
    across = lax.broadcasted_iota(jnp.int32, (rows, rows), 1)
    live = (1 - dead_ref[...]).astype(jnp.float32)
    live = jnp.sum(jnp.where(place == across, live, 0.0), axis=1, keepdims=True)
    copies[1].wait()
    lane = lane_index(rows)
    parts = [[None] * 8, [None] * 8]
    for chunk in range(8):
        product = jnp.dot(
            records_ref[:, chunk * 256 : (chunk + 1) * 256],
            table,
            preferred_element_type=jnp.float32,
        )
        parts[0][chunk] = product[:, :LANES]
        parts[1][chunk] = product[:, LANES:]
    for half in range(2):
        current = parts[half]
        for bit in (1, 2, 4):
            step = 16 * bit
            keep = (lane // step) % 2 == 0
            following = list(current)
            for index in range(8):
                if index & bit == 0:
                    low, high = current[index], current[index | bit]
                    following[index] = jnp.where(keep, low, roll_lanes(high, step))
                    following[index | bit] = jnp.where(keep, roll_lanes(low, -step), high)
            current = following
        for index in range(8):
            staged[pl.ds(half * 8 + index, rows, stride=PITCH), :] = current[index] * live
    for r in range(rows):
        out_ref[r] = staged[pl.ds(r * PITCH, PHASES), :].astype(jnp.bfloat16)


def deal(records, dead_flags):
    rows, length = records.shape
    return pl.pallas_call(
        deal_kernel,
        out_shape=jax.ShapeDtypeStruct((rows, PHASES, LANES), jnp.bfloat16),
        in_specs=[pl.BlockSpec(memory_space=pl.ANY)] * 2,
        out_specs=pl.BlockSpec(memory_space=pltpu.VMEM),
        scratch_shapes=[
            pltpu.VMEM((rows, length), jnp.bfloat16),
            pltpu.VMEM((1, rows), jnp.int32),
            pltpu.VMEM((rows * PITCH, LANES), jnp.float32),
            pltpu.SemaphoreType.DMA((2,)),
        ],
        compiler_params=pltpu.CompilerParams(vmem_limit_bytes=16 * 1024 * 1024),
    )(records, dead_flags.reshape(1, rows))


def dft4(a, b, c, d):
    (ar, ai), (br, bi), (cr, ci), (dr, di) = a, b, c, d
    sr, si, tr, ti = ar + cr, ai + ci, ar - cr, ai - ci
    ur, ui, vr, vi = br + dr, bi + di, br - dr, bi - di
    return [(sr + ur, si + ui), (tr + vi, ti - vr), (sr - ur, si - ui), (tr - vi, ti + vr)]


def rotate(value, power):
    re, im = value
    power %= 16
    if power == 0:
        return value
    if power == 4:
        return (im, -re)
    root = math.sqrt(0.5)
    if power == 2:
        return ((re + im) * root, (im - re) * root)
    if power == 6:
        return ((im - re) * root, (re + im) * (-root))
    cos, sin = math.cos(2 * math.pi * power / 16), math.sin(2 * math.pi * power / 16)
    return (re * cos + im * sin, im * cos - re * sin)


def dft16(values):
    inner = [dft4(values[q], values[q + 4], values[q + 8], values[q + 12]) for q in range(4)]
    result = [None] * 16
    for k in range(4):
        outer = dft4(*[rotate(inner[q][k], q * k) for q in range(4)])
        for j in range(4):
            result[k + 4 * j] = outer[j]
    return result


def stack_kernel(
    starts_ref,
    parts_ref,
    shift_ref,
    high_ref,
    low_ref,
    twiddle_ref,
    middle_ref,
    box_ref,
    inverse_ref,
    flip_ref,
    out_ref,
    plain,
    levels,
    moved,
    normed,
    segments,
    samples,
    factor,
    middles,
    spectrum,
    power,
    smooth,
    folded,
):
    lane = lane_index()
    shards = parts_ref.shape[0]
    for k in range(shards):
        for r in range(ROWS):
            plain[k, pl.ds(r * PITCH, PHASES), :] = parts_ref[k, r].astype(jnp.float32)

    none = jnp.zeros((PHASES * ROWS, LANES), jnp.bfloat16)
    levels[0] = none
    levels[shards + 1] = none
    totals = []
    for k in range(shards):
        level = [jnp.abs(plain[k, pl.ds(p, ROWS, stride=PITCH), :]) for p in range(PHASES)]
        totals.append(functools.reduce(lambda a, b: a + b, level))
        levels[k + 1] = jnp.concatenate(level, axis=0).astype(jnp.bfloat16)
    pairs = jnp.concatenate([levels[: shards + 1], levels[1:]], axis=2)
    pairs = pairs.reshape((shards + 1) * PHASES * ROWS, 2 * LANES)
    product = jnp.dot(pairs, shift_ref[...], preferred_element_type=jnp.float32)
    moved[...] = product.reshape(shards + 1, PHASES * ROWS, 2 * LANES)
    zero = jnp.zeros((ROWS, LANES), jnp.float32)

    def ahead(tiles, by):
        rolled = [roll_lanes(tile, -by) for tile in tiles] + [zero]
        return [jnp.where(lane < LANES - by, rolled[k], rolled[k + 1]) for k in range(len(tiles))]

    def behind(tiles, by):
        rolled = [zero] + [roll_lanes(tile, by) for tile in tiles]
        return [jnp.where(lane >= by, rolled[k + 1], rolled[k]) for k in range(len(tiles))]

    def plus(*lists):
        return [functools.reduce(lambda a, b: a + b, group) for group in zip(*lists)]

    two = plus(totals, ahead(totals, 1))
    four = plus(two, ahead(two, 2))
    columns = plus(ahead(four, 1), ahead(two, 5), ahead(totals, 7))
    past = totals
    for by in (1, 2, 4):
        past = plus(past, behind(past, by))
    columns = plus(columns, past)
    for k in range(shards):
        running = zero
        after = [None] * PHASES
        for p in reversed(range(PHASES)):
            running = running + moved[k, pl.ds(p * ROWS, ROWS), pl.ds(0, LANES)]
            after[p] = running
        running = columns[k]
        for p in range(PHASES):
            total = running + after[p]
            running = running + moved[k + 1, pl.ds(p * ROWS, ROWS), pl.ds(LANES, LANES)]
            if k in (0, shards - 1):
                place = p + PHASES * (k * LANES + lane)
                count = jnp.minimum(place + RMW // 2, NT) - jnp.maximum(place - RMW // 2, 0)
                mean_level = total / count.astype(jnp.float32)
            else:
                mean_level = total * (1.0 / RMW)
            signal = plain[k, pl.ds(p, ROWS, stride=PITCH), :]
            ratio = signal / (mean_level + epsilon)
            normed[p, k] = ratio.astype(jnp.bfloat16).astype(jnp.float32)

    def cut(w, carry):
        start = starts_ref[w]
        phase = start & (PHASES - 1)
        column = start >> 4
        tile = (column >> 8) * 2
        first = column & 255
        for p in range(PHASES):
            least = first + (p < phase).astype(jnp.int32)
            for half in range(2):
                keep = lane >= least - half * LANES
                joined = jnp.where(keep, normed[p, tile + half], normed[p, tile + 2 + half])
                segments[2 * p + half, pl.ds(w, ROWS, stride=NWIN + 1), :] = joined
        return carry

    lax.fori_loop(0, NWIN, cut, 0, unroll=4)

    for n1 in range(PHASES):
        for r in range(ROWS):
            both = jnp.concatenate(
                [segments[2 * n1 + h, pl.ds(r * (NWIN + 1), NWIN), :] for h in range(2)], axis=1
            )
            samples[n1, pl.ds(r * NWIN, NWIN), :] = both.astype(jnp.bfloat16)
    left = samples[...].reshape(PHASES * SEGS, 2 * LANES)
    product = jnp.dot(left, high_ref[...], preferred_element_type=jnp.float32)
    product = product + jnp.dot(left, low_ref[...], preferred_element_type=jnp.float32)
    factor[...] = product.reshape(PHASES, SEGS, 2 * LANES)
    left = jnp.concatenate([samples[n1] for n1 in range(PHASES)], axis=1)
    middles[...] = jnp.dot(
        left, middle_ref[...].reshape(WIN, LANES), preferred_element_type=jnp.float32
    )

    zero_pair = jnp.zeros((SEGS, LANES), jnp.bfloat16)
    power[:, pl.ds(0, LANES)] = zero_pair
    power[:, pl.ds((2 * GROUPS + 1) * LANES, LANES)] = zero_pair

    def combine(pair, carry):
        powers = []
        for part in range(2):
            rows = pl.ds(pl.multiple_of(pair * 16 + part * ROWS, ROWS), ROWS)
            values = []
            for n1 in range(PHASES):
                re, im = factor[n1, rows, pl.ds(0, LANES)], factor[n1, rows, pl.ds(LANES, LANES)]
                if n1:
                    cos, sin = twiddle_ref[2 * n1], twiddle_ref[2 * n1 + 1]
                    re, im = re * cos + im * sin, im * cos - re * sin
                values.append((re, im))
            values = dft16(values)
            centre = middles[rows, :]
            centre = centre + roll_lanes(centre, -16)
            squares = []
            for g in range(GROUPS):
                for side in range(2):
                    re, im = values[15 - g] if side else values[g]
                    if side:
                        re = jnp.where(lane == 0, roll_lanes(centre, -g), re)
                        im = jnp.where(lane == 0, roll_lanes(centre, -(GROUPS + g)), im)
                    spectrum[4 * g + 2 * side, rows, :] = re
                    spectrum[4 * g + 2 * side + 1, rows, :] = im
                    squares.append(re * re + im * im)
            powers.append(squares)
        both = pl.ds(pl.multiple_of(pair * 16, 16), 16)
        for tile in range(2 * GROUPS):
            joined = jnp.concatenate([powers[0][tile], powers[1][tile]], axis=0)
            power[both, pl.ds((tile + 1) * LANES, LANES)] = joined.astype(jnp.bfloat16)
        return carry

    lax.fori_loop(0, SEGS // 16, combine, 0, unroll=4)

    for g in range(GROUPS):
        smooth[...] = jnp.dot(
            power[:, g * 256 : g * 256 + 512], box_ref[...], preferred_element_type=jnp.float32
        )
        for side in range(2):
            inverse = inverse_ref[2 * g + side]
            for c in range(2):
                sums = None
                for octet in range(NWIN // 8):
                    white = []
                    for o in range(NOFF):
                        rows = pl.ds((2 * o + c) * NWIN + octet * 8, 8)
                        level = smooth[rows, side * LANES : (side + 1) * LANES] * inverse
                        scale = lax.rsqrt(level + epsilon)
                        re = spectrum[4 * g + 2 * side, rows, :] * scale
                        im = spectrum[4 * g + 2 * side + 1, rows, :] * scale
                        white.append((re, im))
                    own_re, own_im = white[0]
                    terms = [own_re * own_re + own_im * own_im]
                    for far_re, far_im in white[1:]:
                        terms.append(own_re * far_re + own_im * far_im)
                        if side:
                            terms.append(own_re * far_im - own_im * far_re)
                        else:
                            terms.append(own_im * far_re - own_re * far_im)
                    sums = terms if sums is None else [a + b for a, b in zip(sums, terms)]
                sums = [jnp.sum(x, axis=0, keepdims=True) * (1.0 / NWIN) for x in sums]
                real = jnp.concatenate([sums[0], sums[1], sums[3], sums[5]], axis=0)
                nothing = jnp.zeros((1, LANES), jnp.float32)
                imag = jnp.concatenate([nothing, sums[2], sums[4], sums[6]], axis=0)
                if side:
                    folded[pl.ds((g * 2 + c) * 8, 4), :] = real
                    folded[pl.ds((g * 2 + c) * 8 + 4, 4), :] = imag
                else:
                    out_ref[c, :, pl.ds(g * 256, LANES)] = real
                    out_ref[c, :, pl.ds(NF + g * 256, LANES)] = imag
    folded[...] = jnp.dot(
        folded[...],
        flip_ref[...],
        preferred_element_type=jnp.float32,
        precision=lax.Precision.HIGHEST,
    )
    for g in range(GROUPS):
        for c in range(2):
            row = (g * 2 + c) * 8
            out_ref[c, :, pl.ds(g * 256 + LANES, LANES)] = folded[pl.ds(row, 4), :]
            out_ref[c, :, pl.ds(NF + g * 256 + LANES, LANES)] = folded[pl.ds(row + 4, 4), :]


def stack(parts, starts):
    shards = parts.shape[0]
    vmem = pl.BlockSpec(memory_space=pltpu.VMEM)
    f32 = jnp.float32
    return pl.pallas_call(
        stack_kernel,
        out_shape=jax.ShapeDtypeStruct((2, NOFF, 2 * NF), f32),
        in_specs=[pl.BlockSpec(memory_space=pltpu.SMEM)] + [vmem] * 9,
        out_specs=vmem,
        scratch_shapes=[
            pltpu.VMEM((shards, ROWS * PITCH, LANES), f32),
            pltpu.VMEM((shards + 2, PHASES * ROWS, LANES), jnp.bfloat16),
            pltpu.VMEM((shards + 1, PHASES * ROWS, 2 * LANES), f32),
            pltpu.VMEM((PHASES, shards + 2, ROWS, LANES), f32),
            pltpu.VMEM((2 * PHASES, ROWS * (NWIN + 1), LANES), f32),
            pltpu.VMEM((PHASES, SEGS, 2 * LANES), jnp.bfloat16),
            pltpu.VMEM((PHASES, SEGS, 2 * LANES), f32),
            pltpu.VMEM((SEGS, LANES), f32),
            pltpu.VMEM((4 * GROUPS, SEGS, LANES), f32),
            pltpu.VMEM((SEGS, (2 * GROUPS + 2) * LANES), jnp.bfloat16),
            pltpu.VMEM((SEGS, 2 * LANES), f32),
            pltpu.VMEM((2 * GROUPS * 8, LANES), f32),
        ],
        compiler_params=pltpu.CompilerParams(vmem_limit_bytes=40 * 1024 * 1024),
    )(starts, parts, *[jnp.asarray(table) for table in tables()])


def ahead_on(array, axis, by):
    size = lax.axis_size(axis)
    return lax.ppermute(array, axis, [((i + by) % size, i) for i in range(size)])


def body(records, dead_flags, starts, offsets):
    rows = records.shape[0]
    dealt = deal(records, dead_flags)
    reach = lax.axis_size("loop") // 2
    blocks = [dealt] + [ahead_on(dealt, "loop", by) for by in range(1, reach + 1)]
    nearby = jnp.concatenate(blocks, axis=0)
    members = lax.axis_size("chan")
    picked = [
        lax.dynamic_slice_in_dim(nearby, offsets[o], rows, 0).reshape(
            members, rows // members, PHASES, LANES
        )
        for o in range(NOFF)
    ]
    outgoing = jnp.concatenate(picked, axis=1)
    parts = lax.all_to_all(outgoing, "chan", split_axis=0, concat_axis=0, tiled=True)
    return stack(parts, starts)


def solution(mesh):
    in_specs = (P("loop", "chan"), P("loop"), P(), P())
    out_specs = P(("loop", "chan"), None, None)
    return jax.shard_map(body, mesh=mesh, in_specs=in_specs, out_specs=out_specs, check_vma=False)
```

```python
import functools
import math

import jax
import jax.numpy as jnp
import ml_dtypes
import numpy as np
from jax import lax
from jax.experimental import pallas as pl
from jax.experimental.pallas import tpu as pltpu
from jax.sharding import PartitionSpec as P

NT = 32768
NF = 2048
NWIN = 32
NOFF = 4
RMW = 256
WB = 128
WIN = 4096
LANES = 128
PHASES = 16
PITCH = PHASES + 1
ROWS = 8
SEGS = ROWS * NWIN
GROUPS = NF // 256

epsilon = 1e-06


def split_table(table):
    high = table.astype(ml_dtypes.bfloat16)
    low = (table - high.astype(np.float64)).astype(ml_dtypes.bfloat16)
    return high, low


@functools.lru_cache(maxsize=None)
def tables():
    n2 = np.arange(256)[:, None]
    f2 = np.arange(LANES)[None, :]
    angle = 2.0 * math.pi * ((n2 * f2) % 256) / 256.0
    first = np.concatenate([np.cos(angle), -np.sin(angle)], axis=1)
    first_high, first_low = split_table(first)

    n1 = np.arange(PHASES)[:, None]
    angle = 2.0 * math.pi * ((n1 * f2) % WIN) / WIN
    twiddle = np.stack([np.cos(angle), np.sin(angle)], axis=1)
    twiddle = np.broadcast_to(twiddle[:, :, None, :], (PHASES, 2, ROWS, LANES))
    twiddle = np.ascontiguousarray(twiddle.reshape(2 * PHASES, ROWS, LANES)).astype(np.float32)

    sample = (np.arange(PHASES)[:, None] + PHASES * np.arange(256)[None, :])[:, :, None]
    group = np.arange(GROUPS)[None, None, :]
    angle = 2.0 * math.pi * (((1 + 2 * group) * sample) % 32) / 32.0
    middle = np.concatenate([np.cos(angle), np.sin(angle)], axis=2)
    high, low = split_table(middle)
    middle = np.zeros((PHASES, 256, LANES), ml_dtypes.bfloat16)
    middle[:, :, :16] = high
    middle[:, :, 16:32] = low

    lane = np.arange(LANES)
    upper = np.where(lane == 0, 128, 256 - lane)
    rows = np.concatenate([upper - 256, lane, upper, lane + 256])[:, None]
    columns = np.concatenate([lane, upper])[None, :]
    box = ((rows >= columns - WB // 2) & (rows < columns + WB // 2)).astype(ml_dtypes.bfloat16)

    bins = np.arange(GROUPS)[:, None] * 256 + np.concatenate([lane, upper])[None, :]
    count = np.minimum(bins + WB // 2, NF) - np.maximum(bins - WB // 2, 0)
    inverse = (1.0 / count).astype(np.float32).reshape(2 * GROUPS, 1, LANES)
    inverse = np.ascontiguousarray(np.broadcast_to(inverse, (2 * GROUPS, ROWS, LANES)))

    flip = np.zeros((LANES, LANES), np.float32)
    flip[(LANES - lane) % LANES, lane] = 1.0
    row = np.arange(2 * LANES)[:, None]
    shift = np.concatenate([row == 120 + lane[None, :], row == 8 + lane[None, :]], axis=1)
    shift = shift.astype(ml_dtypes.bfloat16)
    return shift, first_high, first_low, twiddle, middle, box, inverse, flip


def lane_index(rows=ROWS):
    return lax.broadcasted_iota(jnp.int32, (rows, LANES), 1)


def roll_lanes(value, by):
    return pltpu.roll(value, by % LANES, 1)


def deal_kernel(records_hbm, dead_hbm, out_ref, records_ref, dead_ref, staged, sems):
    rows = records_hbm.shape[0]
    copies = [
        pltpu.make_async_copy(dead_hbm, dead_ref, sems.at[0]),
        pltpu.make_async_copy(records_hbm, records_ref, sems.at[1]),
    ]
    for copy in copies:
        copy.start()
    source = lax.broadcasted_iota(jnp.int32, (256, 256), 0)
    target = lax.broadcasted_iota(jnp.int32, (256, 256), 1)
    table = (source == (target % 16) * 16 + target // 16).astype(jnp.bfloat16)
    copies[0].wait()
    place = lax.broadcasted_iota(jnp.int32, (rows, rows), 0)
    across = lax.broadcasted_iota(jnp.int32, (rows, rows), 1)
    live = (1 - dead_ref[...]).astype(jnp.float32)
    live = jnp.sum(jnp.where(place == across, live, 0.0), axis=1, keepdims=True)
    copies[1].wait()
    lane = lane_index(rows)
    parts = [[None] * 8, [None] * 8]
    for chunk in range(8):
        product = jnp.dot(
            records_ref[:, chunk * 256 : (chunk + 1) * 256],
            table,
            preferred_element_type=jnp.float32,
        )
        parts[0][chunk] = product[:, :LANES]
        parts[1][chunk] = product[:, LANES:]
    for half in range(2):
        current = parts[half]
        for bit in (1, 2, 4):
            step = 16 * bit
            keep = (lane // step) % 2 == 0
            following = list(current)
            for index in range(8):
                if index & bit == 0:
                    low, high = current[index], current[index | bit]
                    following[index] = jnp.where(keep, low, roll_lanes(high, step))
                    following[index | bit] = jnp.where(keep, roll_lanes(low, -step), high)
            current = following
        for index in range(8):
            staged[pl.ds(half * 8 + index, rows, stride=PITCH), :] = current[index] * live
    for r in range(rows):
        out_ref[r] = staged[pl.ds(r * PITCH, PHASES), :].astype(jnp.bfloat16)


def deal(records, dead_flags):
    rows, length = records.shape
    return pl.pallas_call(
        deal_kernel,
        out_shape=jax.ShapeDtypeStruct((rows, PHASES, LANES), jnp.bfloat16),
        in_specs=[pl.BlockSpec(memory_space=pltpu.HBM)] * 2,
        out_specs=pl.BlockSpec(memory_space=pltpu.VMEM),
        scratch_shapes=[
            pltpu.VMEM((rows, length), jnp.bfloat16),
            pltpu.VMEM((1, rows), jnp.int32),
            pltpu.VMEM((rows * PITCH, LANES), jnp.float32),
            pltpu.SemaphoreType.DMA((2,)),
        ],
        compiler_params=pltpu.CompilerParams(vmem_limit_bytes=16 * 1024 * 1024),
    )(records, dead_flags.reshape(1, rows))


def dft4(a, b, c, d):
    (ar, ai), (br, bi), (cr, ci), (dr, di) = a, b, c, d
    sr, si, tr, ti = ar + cr, ai + ci, ar - cr, ai - ci
    ur, ui, vr, vi = br + dr, bi + di, br - dr, bi - di
    return [(sr + ur, si + ui), (tr + vi, ti - vr), (sr - ur, si - ui), (tr - vi, ti + vr)]


def rotate(value, power):
    re, im = value
    power %= 16
    if power == 0:
        return value
    if power == 4:
        return (im, -re)
    root = math.sqrt(0.5)
    if power == 2:
        return ((re + im) * root, (im - re) * root)
    if power == 6:
        return ((im - re) * root, (re + im) * (-root))
    cos, sin = math.cos(2 * math.pi * power / 16), math.sin(2 * math.pi * power / 16)
    return (re * cos + im * sin, im * cos - re * sin)


def dft16(values):
    inner = [dft4(values[q], values[q + 4], values[q + 8], values[q + 12]) for q in range(4)]
    result = [None] * 16
    for k in range(4):
        outer = dft4(*[rotate(inner[q][k], q * k) for q in range(4)])
        for j in range(4):
            result[k + 4 * j] = outer[j]
    return result


def stack_kernel(
    starts_ref,
    parts_ref,
    shift_ref,
    high_ref,
    low_ref,
    twiddle_ref,
    middle_ref,
    box_ref,
    inverse_ref,
    flip_ref,
    out_ref,
    plain,
    levels,
    moved,
    normed,
    segments,
    samples,
    factor,
    middles,
    spectrum,
    power,
    smooth,
    folded,
    turned,
):
    lane = lane_index()
    shards = parts_ref.shape[0]
    for k in range(shards):
        for r in range(ROWS):
            plain[k, pl.ds(r * PITCH, PHASES), :] = parts_ref[k, r].astype(jnp.float32)

    none = jnp.zeros((PHASES * ROWS, LANES), jnp.bfloat16)
    levels[0] = none
    levels[shards + 1] = none
    totals = []
    for k in range(shards):
        level = [jnp.abs(plain[k, pl.ds(p, ROWS, stride=PITCH), :]) for p in range(PHASES)]
        totals.append(functools.reduce(lambda a, b: a + b, level))
        levels[k + 1] = jnp.concatenate(level, axis=0).astype(jnp.bfloat16)
    pairs = jnp.concatenate([levels[: shards + 1], levels[1:]], axis=2)
    pairs = pairs.reshape((shards + 1) * PHASES * ROWS, 2 * LANES)
    product = jnp.dot(pairs, shift_ref[...], preferred_element_type=jnp.float32)
    moved[...] = product.reshape(shards + 1, PHASES * ROWS, 2 * LANES)
    zero = jnp.zeros((ROWS, LANES), jnp.float32)

    def ahead(tiles, by):
        rolled = [roll_lanes(tile, -by) for tile in tiles] + [zero]
        return [jnp.where(lane < LANES - by, rolled[k], rolled[k + 1]) for k in range(len(tiles))]

    def behind(tiles, by):
        rolled = [zero] + [roll_lanes(tile, by) for tile in tiles]
        return [jnp.where(lane >= by, rolled[k + 1], rolled[k]) for k in range(len(tiles))]

    def plus(*lists):
        return [functools.reduce(lambda a, b: a + b, group) for group in zip(*lists)]

    two = plus(totals, ahead(totals, 1))
    four = plus(two, ahead(two, 2))
    columns = plus(ahead(four, 1), ahead(two, 5), ahead(totals, 7))
    past = totals
    for by in (1, 2, 4):
        past = plus(past, behind(past, by))
    columns = plus(columns, past)
    for k in range(shards):
        running = zero
        after = [None] * PHASES
        for p in reversed(range(PHASES)):
            running = running + moved[k, pl.ds(p * ROWS, ROWS), pl.ds(0, LANES)]
            after[p] = running
        running = columns[k]
        for p in range(PHASES):
            total = running + after[p]
            running = running + moved[k + 1, pl.ds(p * ROWS, ROWS), pl.ds(LANES, LANES)]
            if k in (0, shards - 1):
                place = p + PHASES * (k * LANES + lane)
                count = jnp.minimum(place + RMW // 2, NT) - jnp.maximum(place - RMW // 2, 0)
                mean_level = total / count.astype(jnp.float32)
            else:
                mean_level = total * (1.0 / RMW)
            signal = plain[k, pl.ds(p, ROWS, stride=PITCH), :]
            ratio = signal / (mean_level + epsilon)
            normed[p, k] = ratio.astype(jnp.bfloat16).astype(jnp.float32)

    place = lane * PHASES

    def cut(w, carry):
        start = starts_ref[w]
        tile = (start >> 12) * 2
        first = start & (WIN - 1)
        for p in range(PHASES):
            for half in range(2):
                keep = place >= first - (half * LANES * PHASES + p)
                joined = jnp.where(keep, normed[p, tile + half], normed[p, tile + 2 + half])
                segments[2 * p + half, pl.ds(w, ROWS, stride=NWIN + 1), :] = joined
        return carry

    lax.fori_loop(0, NWIN, cut, 0, unroll=4)

    for n1 in range(PHASES):
        for r in range(ROWS):
            both = jnp.concatenate(
                [segments[2 * n1 + h, pl.ds(r * (NWIN + 1), NWIN), :] for h in range(2)], axis=1
            )
            samples[n1, pl.ds(r * NWIN, NWIN), :] = both.astype(jnp.bfloat16)
    for n1 in range(0, PHASES, 4):
        left = samples[n1 : n1 + 4].reshape(4 * SEGS, 2 * LANES)
        product = jnp.dot(left, high_ref[...], preferred_element_type=jnp.float32)
        product = product + jnp.dot(left, low_ref[...], preferred_element_type=jnp.float32)
        factor[n1 : n1 + 4] = product.reshape(4, SEGS, 2 * LANES)
    left = jnp.concatenate([samples[n1] for n1 in range(PHASES)], axis=1)
    middles[...] = jnp.dot(
        left, middle_ref[...].reshape(WIN, LANES), preferred_element_type=jnp.float32
    )

    zero_pair = jnp.zeros((SEGS, LANES), jnp.bfloat16)
    power[:, pl.ds(0, LANES)] = zero_pair
    power[:, pl.ds((2 * GROUPS + 1) * LANES, LANES)] = zero_pair

    def combine(pair, carry):
        powers = []
        for part in range(2):
            rows = pl.ds(pl.multiple_of(pair * 16 + part * ROWS, ROWS), ROWS)
            values = []
            for n1 in range(PHASES):
                re, im = factor[n1, rows, pl.ds(0, LANES)], factor[n1, rows, pl.ds(LANES, LANES)]
                if n1:
                    cos, sin = twiddle_ref[2 * n1], twiddle_ref[2 * n1 + 1]
                    re, im = re * cos + im * sin, im * cos - re * sin
                values.append((re, im))
            values = dft16(values)
            centre = middles[rows, :]
            centre = centre + roll_lanes(centre, -16)
            squares = []
            for g in range(GROUPS):
                for side in range(2):
                    re, im = values[15 - g] if side else values[g]
                    if side:
                        re = jnp.where(lane == 0, roll_lanes(centre, -g), re)
                        im = jnp.where(lane == 0, roll_lanes(centre, -(GROUPS + g)), im)
                    spectrum[4 * g + 2 * side, rows, :] = re
                    spectrum[4 * g + 2 * side + 1, rows, :] = im
                    squares.append(re * re + im * im)
            powers.append(squares)
        both = pl.ds(pl.multiple_of(pair * 16, 16), 16)
        for tile in range(2 * GROUPS):
            joined = jnp.concatenate([powers[0][tile], powers[1][tile]], axis=0)
            power[both, pl.ds((tile + 1) * LANES, LANES)] = joined.astype(jnp.bfloat16)
        return carry

    lax.fori_loop(0, SEGS // 16, combine, 0, unroll=4)

    for g in range(GROUPS):
        smooth[g] = jnp.dot(
            power[:, g * 256 : g * 256 + 512], box_ref[...], preferred_element_type=jnp.float32
        )
        for side in range(2):
            inverse = inverse_ref[2 * g + side]
            for c in range(2):
                sums = None
                for octet in range(NWIN // 8):
                    white = []
                    for o in range(NOFF):
                        rows = pl.ds((2 * o + c) * NWIN + octet * 8, 8)
                        level = smooth[g, rows, pl.ds(side * LANES, LANES)] * inverse
                        scale = lax.rsqrt(level + epsilon)
                        re = spectrum[4 * g + 2 * side, rows, :] * scale
                        im = spectrum[4 * g + 2 * side + 1, rows, :] * scale
                        white.append((re, im))
                    own_re, own_im = white[0]
                    terms = [own_re * own_re + own_im * own_im]
                    for far_re, far_im in white[1:]:
                        terms.append(own_re * far_re + own_im * far_im)
                        if side:
                            terms.append(own_re * far_im - own_im * far_re)
                        else:
                            terms.append(own_im * far_re - own_re * far_im)
                    sums = terms if sums is None else [a + b for a, b in zip(sums, terms)]
                place = (2 * g + side) * 2 + c
                rows = [sums[0], sums[1], sums[3], sums[5], zero, sums[2], sums[4], sums[6]]
                for index, value in enumerate(rows):
                    turned[place, pl.ds(index, 8, stride=9), :] = value
                result = [turned[place, pl.ds(9 * index, 8), :] for index in range(8)]
                result = functools.reduce(lambda a, b: a + b, result) * (1.0 / NWIN)
                if side:
                    folded[pl.ds((g * 2 + c) * 8, 8), :] = result
                else:
                    out_ref[c, :, pl.ds(g * 256, LANES)] = result[:NOFF]
                    out_ref[c, :, pl.ds(NF + g * 256, LANES)] = result[NOFF:]
    folded[...] = jnp.dot(
        folded[...],
        flip_ref[...],
        preferred_element_type=jnp.float32,
        precision=lax.Precision.HIGHEST,
    )
    for g in range(GROUPS):
        for c in range(2):
            row = (g * 2 + c) * 8
            out_ref[c, :, pl.ds(g * 256 + LANES, LANES)] = folded[pl.ds(row, 4), :]
            out_ref[c, :, pl.ds(NF + g * 256 + LANES, LANES)] = folded[pl.ds(row + 4, 4), :]


def stack(parts, starts):
    shards = parts.shape[0]
    vmem = pl.BlockSpec(memory_space=pltpu.VMEM)
    f32 = jnp.float32
    return pl.pallas_call(
        stack_kernel,
        out_shape=jax.ShapeDtypeStruct((2, NOFF, 2 * NF), f32),
        in_specs=[pl.BlockSpec(memory_space=pltpu.SMEM)] + [vmem] * 9,
        out_specs=vmem,
        scratch_shapes=[
            pltpu.VMEM((shards, ROWS * PITCH, LANES), f32),
            pltpu.VMEM((shards + 2, PHASES * ROWS, LANES), jnp.bfloat16),
            pltpu.VMEM((shards + 1, PHASES * ROWS, 2 * LANES), f32),
            pltpu.VMEM((PHASES, shards + 2, ROWS, LANES), f32),
            pltpu.VMEM((2 * PHASES, ROWS * (NWIN + 1), LANES), f32),
            pltpu.VMEM((PHASES, SEGS, 2 * LANES), jnp.bfloat16),
            pltpu.VMEM((PHASES, SEGS, 2 * LANES), f32),
            pltpu.VMEM((SEGS, LANES), f32),
            pltpu.VMEM((4 * GROUPS, SEGS, LANES), f32),
            pltpu.VMEM((SEGS, (2 * GROUPS + 2) * LANES), jnp.bfloat16),
            pltpu.VMEM((GROUPS, SEGS, 2 * LANES), f32),
            pltpu.VMEM((2 * GROUPS * 8, LANES), f32),
            pltpu.VMEM((4 * GROUPS, 72, LANES), f32),
        ],
        compiler_params=pltpu.CompilerParams(vmem_limit_bytes=40 * 1024 * 1024),
    )(starts, parts, *[jnp.asarray(table) for table in tables()])


def ahead_on(array, axis, by):
    size = lax.axis_size(axis)
    return lax.ppermute(array, axis, [((i + by) % size, i) for i in range(size)])


def body(records, dead_flags, starts, offsets):
    rows = records.shape[0]
    dealt = deal(records, dead_flags)
    reach = lax.axis_size("loop") // 2
    blocks = [dealt] + [ahead_on(dealt, "loop", by) for by in range(1, reach + 1)]
    nearby = jnp.concatenate(blocks, axis=0)
    members = lax.axis_size("chan")
    picked = [
        lax.dynamic_slice_in_dim(nearby, offsets[o], rows, 0).reshape(
            members, rows // members, PHASES, LANES
        )
        for o in range(NOFF)
    ]
    outgoing = jnp.concatenate(picked, axis=1)
    parts = lax.all_to_all(outgoing, "chan", split_axis=0, concat_axis=0, tiled=True)
    return stack(parts, starts)


def solution(mesh):
    in_specs = (P("loop", "chan"), P("loop"), P(), P())
    out_specs = P(("loop", "chan"), None, None)
    return jax.shard_map(body, mesh=mesh, in_specs=in_specs, out_specs=out_specs, check_vma=False)
```

```python
import functools
import math

import jax
import jax.numpy as jnp
import ml_dtypes
import numpy as np
from jax import lax
from jax.experimental import pallas as pl
from jax.experimental.pallas import tpu as pltpu
from jax.sharding import PartitionSpec as P

NT = 32768
NF = 2048
NWIN = 32
NOFF = 4
RMW = 256
WB = 128
WIN = 4096
LANES = 128
PHASES = 16
PITCH = PHASES + 1
ROWS = 8
SEGS = ROWS * NWIN
GROUPS = NF // 256

epsilon = 1e-06


def split_table(table):
    high = table.astype(ml_dtypes.bfloat16)
    low = (table - high.astype(np.float64)).astype(ml_dtypes.bfloat16)
    return high, low


@functools.lru_cache(maxsize=None)
def tables():
    n2 = np.arange(256)[:, None]
    f2 = np.arange(LANES)[None, :]
    angle = 2.0 * math.pi * ((n2 * f2) % 256) / 256.0
    first = np.concatenate([np.cos(angle), -np.sin(angle)], axis=1)
    first_high, first_low = split_table(first)

    n1 = np.arange(PHASES)[:, None]
    angle = 2.0 * math.pi * ((n1 * f2) % WIN) / WIN
    twiddle = np.stack([np.cos(angle), np.sin(angle)], axis=1)
    twiddle = np.broadcast_to(twiddle[:, :, None, :], (PHASES, 2, ROWS, LANES))
    twiddle = np.ascontiguousarray(twiddle.reshape(2 * PHASES, ROWS, LANES)).astype(np.float32)

    sample = (np.arange(PHASES)[:, None] + PHASES * np.arange(256)[None, :])[:, :, None]
    group = np.arange(GROUPS)[None, None, :]
    angle = 2.0 * math.pi * (((1 + 2 * group) * sample) % 32) / 32.0
    middle = np.concatenate([np.cos(angle), np.sin(angle)], axis=2)
    high, low = split_table(middle)
    middle = np.zeros((PHASES, 256, LANES), ml_dtypes.bfloat16)
    middle[:, :, :16] = high
    middle[:, :, 16:32] = low

    lane = np.arange(LANES)
    upper = np.where(lane == 0, 128, 256 - lane)
    rows = np.concatenate([upper - 256, lane, upper, lane + 256])[:, None]
    columns = np.concatenate([lane, upper])[None, :]
    box = ((rows >= columns - WB // 2) & (rows < columns + WB // 2)).astype(ml_dtypes.bfloat16)

    bins = np.arange(GROUPS)[:, None] * 256 + np.concatenate([lane, upper])[None, :]
    count = np.minimum(bins + WB // 2, NF) - np.maximum(bins - WB // 2, 0)
    inverse = (1.0 / count).astype(np.float32).reshape(2 * GROUPS, 1, LANES)
    inverse = np.ascontiguousarray(np.broadcast_to(inverse, (2 * GROUPS, ROWS, LANES)))

    flip = np.zeros((LANES, LANES), np.float32)
    flip[(LANES - lane) % LANES, lane] = 1.0
    row = np.arange(2 * LANES)[:, None]
    shift = np.concatenate([row == 120 + lane[None, :], row == 8 + lane[None, :]], axis=1)
    shift = shift.astype(ml_dtypes.bfloat16)
    return shift, first_high, first_low, twiddle, middle, box, inverse, flip


def lane_index(rows=ROWS):
    return lax.broadcasted_iota(jnp.int32, (rows, LANES), 1)


def roll_lanes(value, by):
    return pltpu.roll(value, by % LANES, 1)


def deal_kernel(records_ref, live_ref, out_ref, staged):
    rows = records_ref.shape[0]
    source = lax.broadcasted_iota(jnp.int32, (256, 256), 0)
    target = lax.broadcasted_iota(jnp.int32, (256, 256), 1)
    table = (source == (target % 16) * 16 + target // 16).astype(jnp.bfloat16)
    place = lax.broadcasted_iota(jnp.int32, (rows, rows), 0)
    across = lax.broadcasted_iota(jnp.int32, (rows, rows), 1)
    live = jnp.where(place == across, live_ref[...], 0.0)
    live = jnp.sum(live, axis=1, keepdims=True)
    lane = lane_index(rows)
    parts = [[None] * 8, [None] * 8]
    for chunk in range(8):
        product = jnp.dot(
            records_ref[:, chunk * 256 : (chunk + 1) * 256],
            table,
            preferred_element_type=jnp.float32,
        )
        parts[0][chunk] = product[:, :LANES]
        parts[1][chunk] = product[:, LANES:]
    for half in range(2):
        current = parts[half]
        for bit in (1, 2, 4):
            step = 16 * bit
            keep = (lane // step) % 2 == 0
            following = list(current)
            for index in range(8):
                if index & bit == 0:
                    low, high = current[index], current[index | bit]
                    following[index] = jnp.where(keep, low, roll_lanes(high, step))
                    following[index | bit] = jnp.where(keep, roll_lanes(low, -step), high)
            current = following
        for index in range(8):
            staged[pl.ds(half * 8 + index, rows, stride=PITCH), :] = current[index] * live
    for r in range(rows):
        out_ref[r] = staged[pl.ds(r * PITCH, PHASES), :].astype(jnp.bfloat16)


def deal(records, dead_flags):
    rows = records.shape[0]
    live = (1 - dead_flags).astype(jnp.float32).reshape(1, rows)
    vmem = pl.BlockSpec(memory_space=pltpu.VMEM)
    return pl.pallas_call(
        deal_kernel,
        out_shape=jax.ShapeDtypeStruct((rows, PHASES, LANES), jnp.bfloat16),
        in_specs=[vmem] * 2,
        out_specs=vmem,
        scratch_shapes=[pltpu.VMEM((rows * PITCH, LANES), jnp.float32)],
        compiler_params=pltpu.CompilerParams(vmem_limit_bytes=16 * 1024 * 1024),
    )(records, live)


def dft4(a, b, c, d):
    (ar, ai), (br, bi), (cr, ci), (dr, di) = a, b, c, d
    sr, si, tr, ti = ar + cr, ai + ci, ar - cr, ai - ci
    ur, ui, vr, vi = br + dr, bi + di, br - dr, bi - di
    return [(sr + ur, si + ui), (tr + vi, ti - vr), (sr - ur, si - ui), (tr - vi, ti + vr)]


def rotate(value, power):
    re, im = value
    power %= 16
    if power == 0:
        return value
    if power == 4:
        return (im, -re)
    root = math.sqrt(0.5)
    if power == 2:
        return ((re + im) * root, (im - re) * root)
    if power == 6:
        return ((im - re) * root, (re + im) * (-root))
    cos, sin = math.cos(2 * math.pi * power / 16), math.sin(2 * math.pi * power / 16)
    return (re * cos + im * sin, im * cos - re * sin)


def dft16(values):
    inner = [dft4(values[q], values[q + 4], values[q + 8], values[q + 12]) for q in range(4)]
    result = [None] * 16
    for k in range(4):
        outer = dft4(*[rotate(inner[q][k], q * k) for q in range(4)])
        for j in range(4):
            result[k + 4 * j] = outer[j]
    return result


def stack_kernel(
    starts_ref,
    parts_ref,
    shift_ref,
    high_ref,
    low_ref,
    twiddle_ref,
    middle_ref,
    box_ref,
    inverse_ref,
    flip_ref,
    out_ref,
    plain,
    levels,
    moved,
    normed,
    segments,
    samples,
    factor,
    middles,
    spectrum,
    power,
    smooth,
    folded,
    turned,
):
    lane = lane_index()
    shards = parts_ref.shape[0]
    for k in range(shards):
        for r in range(ROWS):
            plain[k, pl.ds(r * PITCH, PHASES), :] = parts_ref[k, r].astype(jnp.float32)

    none = jnp.zeros((PHASES * ROWS, LANES), jnp.bfloat16)
    levels[0] = none
    levels[shards + 1] = none
    totals = []
    for k in range(shards):
        level = [jnp.abs(plain[k, pl.ds(p, ROWS, stride=PITCH), :]) for p in range(PHASES)]
        totals.append(functools.reduce(lambda a, b: a + b, level))
        levels[k + 1] = jnp.concatenate(level, axis=0).astype(jnp.bfloat16)
    pairs = jnp.concatenate([levels[: shards + 1], levels[1:]], axis=2)
    pairs = pairs.reshape((shards + 1) * PHASES * ROWS, 2 * LANES)
    product = jnp.dot(pairs, shift_ref[...], preferred_element_type=jnp.float32)
    moved[...] = product.reshape(shards + 1, PHASES * ROWS, 2 * LANES)
    zero = jnp.zeros((ROWS, LANES), jnp.float32)

    def ahead(tiles, by):
        rolled = [roll_lanes(tile, -by) for tile in tiles] + [zero]
        return [jnp.where(lane < LANES - by, rolled[k], rolled[k + 1]) for k in range(len(tiles))]

    def behind(tiles, by):
        rolled = [zero] + [roll_lanes(tile, by) for tile in tiles]
        return [jnp.where(lane >= by, rolled[k + 1], rolled[k]) for k in range(len(tiles))]

    def plus(*lists):
        return [functools.reduce(lambda a, b: a + b, group) for group in zip(*lists)]

    two = plus(totals, ahead(totals, 1))
    four = plus(two, ahead(two, 2))
    columns = plus(ahead(four, 1), ahead(two, 5), ahead(totals, 7))
    past = totals
    for by in (1, 2, 4):
        past = plus(past, behind(past, by))
    columns = plus(columns, past)
    for k in range(shards):
        running = zero
        after = [None] * PHASES
        for p in reversed(range(PHASES)):
            running = running + moved[k, pl.ds(p * ROWS, ROWS), pl.ds(0, LANES)]
            after[p] = running
        running = columns[k]
        for p in range(PHASES):
            total = running + after[p]
            running = running + moved[k + 1, pl.ds(p * ROWS, ROWS), pl.ds(LANES, LANES)]
            if k in (0, shards - 1):
                place = p + PHASES * (k * LANES + lane)
                count = jnp.minimum(place + RMW // 2, NT) - jnp.maximum(place - RMW // 2, 0)
                mean_level = total / count.astype(jnp.float32)
            else:
                mean_level = total * (1.0 / RMW)
            signal = plain[k, pl.ds(p, ROWS, stride=PITCH), :]
            ratio = signal / (mean_level + epsilon)
            normed[p, k] = ratio.astype(jnp.bfloat16).astype(jnp.float32)

    place = lane * PHASES

    def cut(w, carry):
        start = starts_ref[w]
        tile = (start >> 12) * 2
        first = start & (WIN - 1)
        for p in range(PHASES):
            for half in range(2):
                keep = place >= first - (half * LANES * PHASES + p)
                joined = jnp.where(keep, normed[p, tile + half], normed[p, tile + 2 + half])
                segments[2 * p + half, pl.ds(w, ROWS, stride=NWIN + 1), :] = joined
        return carry

    lax.fori_loop(0, NWIN, cut, 0, unroll=4)

    for n1 in range(PHASES):
        for r in range(ROWS):
            both = jnp.concatenate(
                [segments[2 * n1 + h, pl.ds(r * (NWIN + 1), NWIN), :] for h in range(2)], axis=1
            )
            samples[n1, pl.ds(r * NWIN, NWIN), :] = both.astype(jnp.bfloat16)
    for n1 in range(0, PHASES, 4):
        left = samples[n1 : n1 + 4].reshape(4 * SEGS, 2 * LANES)
        product = jnp.dot(left, high_ref[...], preferred_element_type=jnp.float32)
        product = product + jnp.dot(left, low_ref[...], preferred_element_type=jnp.float32)
        factor[n1 : n1 + 4] = product.reshape(4, SEGS, 2 * LANES)
    left = jnp.concatenate([samples[n1] for n1 in range(PHASES)], axis=1)
    middles[...] = jnp.dot(
        left, middle_ref[...].reshape(WIN, LANES), preferred_element_type=jnp.float32
    )

    zero_pair = jnp.zeros((SEGS, LANES), jnp.bfloat16)
    power[:, pl.ds(0, LANES)] = zero_pair
    power[:, pl.ds((2 * GROUPS + 1) * LANES, LANES)] = zero_pair

    def combine(pair, carry):
        powers = []
        for part in range(2):
            rows = pl.ds(pl.multiple_of(pair * 16 + part * ROWS, ROWS), ROWS)
            values = []
            for n1 in range(PHASES):
                re, im = factor[n1, rows, pl.ds(0, LANES)], factor[n1, rows, pl.ds(LANES, LANES)]
                if n1:
                    cos, sin = twiddle_ref[2 * n1], twiddle_ref[2 * n1 + 1]
                    re, im = re * cos + im * sin, im * cos - re * sin
                values.append((re, im))
            values = dft16(values)
            centre = middles[rows, :]
            centre = centre + roll_lanes(centre, -16)
            squares = []
            for g in range(GROUPS):
                for side in range(2):
                    re, im = values[15 - g] if side else values[g]
                    if side:
                        re = jnp.where(lane == 0, roll_lanes(centre, -g), re)
                        im = jnp.where(lane == 0, roll_lanes(centre, -(GROUPS + g)), im)
                    spectrum[4 * g + 2 * side, rows, :] = re
                    spectrum[4 * g + 2 * side + 1, rows, :] = im
                    squares.append(re * re + im * im)
            powers.append(squares)
        both = pl.ds(pl.multiple_of(pair * 16, 16), 16)
        for tile in range(2 * GROUPS):
            joined = jnp.concatenate([powers[0][tile], powers[1][tile]], axis=0)
            power[both, pl.ds((tile + 1) * LANES, LANES)] = joined.astype(jnp.bfloat16)
        return carry

    lax.fori_loop(0, SEGS // 16, combine, 0, unroll=4)

    for g in range(GROUPS):
        smooth[g] = jnp.dot(
            power[:, g * 256 : g * 256 + 512], box_ref[...], preferred_element_type=jnp.float32
        )
        for side in range(2):
            inverse = inverse_ref[2 * g + side]
            for c in range(2):
                sums = None
                for octet in range(NWIN // 8):
                    white = []
                    for o in range(NOFF):
                        rows = pl.ds((2 * o + c) * NWIN + octet * 8, 8)
                        level = smooth[g, rows, pl.ds(side * LANES, LANES)] * inverse
                        scale = lax.rsqrt(level + epsilon)
                        re = spectrum[4 * g + 2 * side, rows, :] * scale
                        im = spectrum[4 * g + 2 * side + 1, rows, :] * scale
                        white.append((re, im))
                    own_re, own_im = white[0]
                    terms = [own_re * own_re + own_im * own_im]
                    for far_re, far_im in white[1:]:
                        terms.append(own_re * far_re + own_im * far_im)
                        if side:
                            terms.append(own_re * far_im - own_im * far_re)
                        else:
                            terms.append(own_im * far_re - own_re * far_im)
                    sums = terms if sums is None else [a + b for a, b in zip(sums, terms)]
                place = (2 * g + side) * 2 + c
                rows = [sums[0], sums[1], sums[3], sums[5], zero, sums[2], sums[4], sums[6]]
                for index, value in enumerate(rows):
                    turned[place, pl.ds(index, 8, stride=9), :] = value
                result = [turned[place, pl.ds(9 * index, 8), :] for index in range(8)]
                result = functools.reduce(lambda a, b: a + b, result) * (1.0 / NWIN)
                if side:
                    folded[pl.ds((g * 2 + c) * 8, 8), :] = result
                else:
                    out_ref[c, :, pl.ds(g * 256, LANES)] = result[:NOFF]
                    out_ref[c, :, pl.ds(NF + g * 256, LANES)] = result[NOFF:]
    folded[...] = jnp.dot(
        folded[...],
        flip_ref[...],
        preferred_element_type=jnp.float32,
        precision=lax.Precision.HIGHEST,
    )
    for g in range(GROUPS):
        for c in range(2):
            row = (g * 2 + c) * 8
            out_ref[c, :, pl.ds(g * 256 + LANES, LANES)] = folded[pl.ds(row, 4), :]
            out_ref[c, :, pl.ds(NF + g * 256 + LANES, LANES)] = folded[pl.ds(row + 4, 4), :]


def stack(parts, starts):
    shards = parts.shape[0]
    vmem = pl.BlockSpec(memory_space=pltpu.VMEM)
    f32 = jnp.float32
    return pl.pallas_call(
        stack_kernel,
        out_shape=jax.ShapeDtypeStruct((2, NOFF, 2 * NF), f32),
        in_specs=[pl.BlockSpec(memory_space=pltpu.SMEM)] + [vmem] * 9,
        out_specs=vmem,
        scratch_shapes=[
            pltpu.VMEM((shards, ROWS * PITCH, LANES), f32),
            pltpu.VMEM((shards + 2, PHASES * ROWS, LANES), jnp.bfloat16),
            pltpu.VMEM((shards + 1, PHASES * ROWS, 2 * LANES), f32),
            pltpu.VMEM((PHASES, shards + 2, ROWS, LANES), f32),
            pltpu.VMEM((2 * PHASES, ROWS * (NWIN + 1), LANES), f32),
            pltpu.VMEM((PHASES, SEGS, 2 * LANES), jnp.bfloat16),
            pltpu.VMEM((PHASES, SEGS, 2 * LANES), f32),
            pltpu.VMEM((SEGS, LANES), f32),
            pltpu.VMEM((4 * GROUPS, SEGS, LANES), f32),
            pltpu.VMEM((SEGS, (2 * GROUPS + 2) * LANES), jnp.bfloat16),
            pltpu.VMEM((GROUPS, SEGS, 2 * LANES), f32),
            pltpu.VMEM((2 * GROUPS * 8, LANES), f32),
            pltpu.VMEM((4 * GROUPS, 72, LANES), f32),
        ],
        compiler_params=pltpu.CompilerParams(vmem_limit_bytes=40 * 1024 * 1024),
    )(starts, parts, *[jnp.asarray(table) for table in tables()])


def ahead_on(array, axis, by):
    size = lax.axis_size(axis)
    return lax.ppermute(array, axis, [((i + by) % size, i) for i in range(size)])


def body(records, dead_flags, starts, offsets):
    rows = records.shape[0]
    dealt = deal(records, dead_flags)
    reach = lax.axis_size("loop") // 2
    blocks = [dealt] + [ahead_on(dealt, "loop", by) for by in range(1, reach + 1)]
    nearby = jnp.concatenate(blocks, axis=0)
    members = lax.axis_size("chan")
    picked = [
        lax.dynamic_slice_in_dim(nearby, offsets[o], rows, 0).reshape(
            members, rows // members, PHASES, LANES
        )
        for o in range(NOFF)
    ]
    outgoing = jnp.concatenate(picked, axis=1)
    parts = lax.all_to_all(outgoing, "chan", split_axis=0, concat_axis=0, tiled=True)
    return stack(parts, starts)


def solution(mesh):
    in_specs = (P("loop", "chan"), P("loop"), P(), P())
    out_specs = P(("loop", "chan"), None, None)
    return jax.shard_map(body, mesh=mesh, in_specs=in_specs, out_specs=out_specs, check_vma=False)
```

```python
import functools
import math

import jax
import jax.numpy as jnp
import ml_dtypes
import numpy as np
from jax import lax
from jax.experimental import pallas as pl
from jax.experimental.pallas import tpu as pltpu
from jax.sharding import PartitionSpec as P

NT = 32768
NF = 2048
NWIN = 32
NOFF = 4
RMW = 256
WB = 128
WIN = 4096
LANES = 128
PHASES = 16
PITCH = PHASES + 1
ROWS = 8
SEGS = ROWS * NWIN
GROUPS = NF // 256

epsilon = 1e-06


def split_table(table):
    high = table.astype(ml_dtypes.bfloat16)
    low = (table - high.astype(np.float64)).astype(ml_dtypes.bfloat16)
    return high, low


@functools.lru_cache(maxsize=None)
def tables():
    n2 = np.arange(256)[:, None]
    f2 = np.arange(LANES)[None, :]
    angle = 2.0 * math.pi * ((n2 * f2) % 256) / 256.0
    first = np.concatenate([np.cos(angle), -np.sin(angle)], axis=1)
    first_high, first_low = split_table(first)

    n1 = np.arange(PHASES)[:, None]
    angle = 2.0 * math.pi * ((n1 * f2) % WIN) / WIN
    twiddle = np.stack([np.cos(angle), np.sin(angle)], axis=1)
    twiddle = np.broadcast_to(twiddle[:, :, None, :], (PHASES, 2, ROWS, LANES))
    twiddle = np.ascontiguousarray(twiddle.reshape(2 * PHASES, ROWS, LANES)).astype(np.float32)

    sample = (np.arange(PHASES)[:, None] + PHASES * np.arange(256)[None, :])[:, :, None]
    group = np.arange(GROUPS)[None, None, :]
    angle = 2.0 * math.pi * (((1 + 2 * group) * sample) % 32) / 32.0
    middle = np.concatenate([np.cos(angle), np.sin(angle)], axis=2)
    high, low = split_table(middle)
    middle = np.zeros((PHASES, 256, LANES), ml_dtypes.bfloat16)
    middle[:, :, :16] = high
    middle[:, :, 16:32] = low

    lane = np.arange(LANES)
    upper = np.where(lane == 0, 128, 256 - lane)
    rows = np.concatenate([upper - 256, lane, upper, lane + 256])[:, None]
    columns = np.concatenate([lane, upper])[None, :]
    box = ((rows >= columns - WB // 2) & (rows < columns + WB // 2)).astype(ml_dtypes.bfloat16)

    bins = np.arange(GROUPS)[:, None] * 256 + np.concatenate([lane, upper])[None, :]
    count = np.minimum(bins + WB // 2, NF) - np.maximum(bins - WB // 2, 0)
    inverse = (1.0 / count).astype(np.float32).reshape(2 * GROUPS, 1, LANES)
    inverse = np.ascontiguousarray(np.broadcast_to(inverse, (2 * GROUPS, ROWS, LANES)))

    flip = np.zeros((LANES, LANES), np.float32)
    flip[(LANES - lane) % LANES, lane] = 1.0
    row = np.arange(2 * LANES)[:, None]
    shift = np.concatenate([row == 120 + lane[None, :], row == 8 + lane[None, :]], axis=1)
    shift = shift.astype(ml_dtypes.bfloat16)
    return shift, first_high, first_low, twiddle, middle, box, inverse, flip


def lane_index(rows=ROWS):
    return lax.broadcasted_iota(jnp.int32, (rows, LANES), 1)


def roll_lanes(value, by):
    return pltpu.roll(value, by % LANES, 1)


def deal_kernel(records_ref, live_ref, out_ref, staged):
    rows = records_ref.shape[0]
    source = lax.broadcasted_iota(jnp.int32, (256, 256), 0)
    target = lax.broadcasted_iota(jnp.int32, (256, 256), 1)
    table = (source == (target % 16) * 16 + target // 16).astype(jnp.bfloat16)
    place = lax.broadcasted_iota(jnp.int32, (rows, rows), 0)
    across = lax.broadcasted_iota(jnp.int32, (rows, rows), 1)
    live = jnp.where(place == across, live_ref[...], 0.0)
    live = jnp.sum(live, axis=1, keepdims=True)
    lane = lane_index(rows)
    parts = [[None] * 8, [None] * 8]
    for chunk in range(8):
        product = jnp.dot(
            records_ref[:, chunk * 256 : (chunk + 1) * 256],
            table,
            preferred_element_type=jnp.float32,
        )
        parts[0][chunk] = product[:, :LANES]
        parts[1][chunk] = product[:, LANES:]
    for half in range(2):
        current = parts[half]
        for bit in (1, 2, 4):
            step = 16 * bit
            keep = (lane // step) % 2 == 0
            following = list(current)
            for index in range(8):
                if index & bit == 0:
                    low, high = current[index], current[index | bit]
                    following[index] = jnp.where(keep, low, roll_lanes(high, step))
                    following[index | bit] = jnp.where(keep, roll_lanes(low, -step), high)
            current = following
        for index in range(8):
            staged[pl.ds(half * 8 + index, rows, stride=PITCH), :] = current[index] * live
    for r in range(rows):
        out_ref[r] = staged[pl.ds(r * PITCH, PHASES), :].astype(jnp.bfloat16)


def deal(records, dead_flags):
    rows = records.shape[0]
    live = (1 - dead_flags).astype(jnp.float32).reshape(1, rows)
    vmem = pl.BlockSpec(memory_space=pltpu.VMEM)
    return pl.pallas_call(
        deal_kernel,
        out_shape=jax.ShapeDtypeStruct((rows, PHASES, LANES), jnp.bfloat16),
        in_specs=[vmem] * 2,
        out_specs=vmem,
        scratch_shapes=[pltpu.VMEM((rows * PITCH, LANES), jnp.float32)],
        compiler_params=pltpu.CompilerParams(vmem_limit_bytes=16 * 1024 * 1024),
    )(records, live)


def dft4(a, b, c, d):
    (ar, ai), (br, bi), (cr, ci), (dr, di) = a, b, c, d
    sr, si, tr, ti = ar + cr, ai + ci, ar - cr, ai - ci
    ur, ui, vr, vi = br + dr, bi + di, br - dr, bi - di
    return [(sr + ur, si + ui), (tr + vi, ti - vr), (sr - ur, si - ui), (tr - vi, ti + vr)]


def rotate(value, power):
    re, im = value
    power %= 16
    if power == 0:
        return value
    if power == 4:
        return (im, -re)
    root = math.sqrt(0.5)
    if power == 2:
        return ((re + im) * root, (im - re) * root)
    if power == 6:
        return ((im - re) * root, (re + im) * (-root))
    cos, sin = math.cos(2 * math.pi * power / 16), math.sin(2 * math.pi * power / 16)
    return (re * cos + im * sin, im * cos - re * sin)


def dft16(values):
    inner = [dft4(values[q], values[q + 4], values[q + 8], values[q + 12]) for q in range(4)]
    result = [None] * 16
    for k in range(4):
        outer = dft4(*[rotate(inner[q][k], q * k) for q in range(4)])
        for j in range(4):
            result[k + 4 * j] = outer[j]
    return result


def stack_kernel(
    starts_ref,
    parts_ref,
    shift_ref,
    high_ref,
    low_ref,
    twiddle_ref,
    middle_ref,
    box_ref,
    inverse_ref,
    flip_ref,
    out_ref,
    plain,
    levels,
    moved,
    normed,
    segments,
    samples,
    factor,
    middles,
    spectrum,
    power,
    smooth,
    folded,
    turned,
):
    lane = lane_index()
    shards = parts_ref.shape[0]
    for k in range(shards):
        for r in range(ROWS):
            plain[k, pl.ds(r * PITCH, PHASES), :] = parts_ref[k, r].astype(jnp.float32)

    none = jnp.zeros((PHASES * ROWS, LANES), jnp.bfloat16)
    levels[0] = none
    levels[shards + 1] = none
    totals = []
    for k in range(shards):
        level = [jnp.abs(plain[k, pl.ds(p, ROWS, stride=PITCH), :]) for p in range(PHASES)]
        totals.append(functools.reduce(lambda a, b: a + b, level))
        levels[k + 1] = jnp.concatenate(level, axis=0).astype(jnp.bfloat16)
    pairs = jnp.concatenate([levels[: shards + 1], levels[1:]], axis=2)
    pairs = pairs.reshape((shards + 1) * PHASES * ROWS, 2 * LANES)
    product = jnp.dot(pairs, shift_ref[...], preferred_element_type=jnp.float32)
    moved[...] = product.reshape(shards + 1, PHASES * ROWS, 2 * LANES)
    zero = jnp.zeros((ROWS, LANES), jnp.float32)

    def ahead(tiles, by):
        rolled = [roll_lanes(tile, -by) for tile in tiles] + [zero]
        return [jnp.where(lane < LANES - by, rolled[k], rolled[k + 1]) for k in range(len(tiles))]

    def behind(tiles, by):
        rolled = [zero] + [roll_lanes(tile, by) for tile in tiles]
        return [jnp.where(lane >= by, rolled[k + 1], rolled[k]) for k in range(len(tiles))]

    def plus(*lists):
        return [functools.reduce(lambda a, b: a + b, group) for group in zip(*lists)]

    two = plus(totals, ahead(totals, 1))
    four = plus(two, ahead(two, 2))
    columns = plus(ahead(four, 1), ahead(two, 5), ahead(totals, 7))
    past = totals
    for by in (1, 2, 4):
        past = plus(past, behind(past, by))
    columns = plus(columns, past)
    for k in range(shards):
        running = zero
        after = [None] * PHASES
        for p in reversed(range(PHASES)):
            running = running + moved[k, pl.ds(p * ROWS, ROWS), pl.ds(0, LANES)]
            after[p] = running
        running = columns[k]
        for p in range(PHASES):
            total = running + after[p]
            running = running + moved[k + 1, pl.ds(p * ROWS, ROWS), pl.ds(LANES, LANES)]
            if k in (0, shards - 1):
                place = p + PHASES * (k * LANES + lane)
                count = jnp.minimum(place + RMW // 2, NT) - jnp.maximum(place - RMW // 2, 0)
                mean_level = total / count.astype(jnp.float32)
            else:
                mean_level = total * (1.0 / RMW)
            signal = plain[k, pl.ds(p, ROWS, stride=PITCH), :]
            ratio = signal / (mean_level + epsilon)
            normed[p, k] = ratio.astype(jnp.bfloat16).astype(jnp.float32)

    place = lane * PHASES

    def cut(w, carry):
        start = starts_ref[w]
        tile = (start >> 12) * 2
        first = start & (WIN - 1)
        for p in range(PHASES):
            for half in range(2):
                keep = place >= first - (half * LANES * PHASES + p)
                joined = jnp.where(keep, normed[p, tile + half], normed[p, tile + 2 + half])
                segments[2 * p + half, pl.ds(w, ROWS, stride=NWIN + 1), :] = joined
        return carry

    lax.fori_loop(0, NWIN, cut, 0, unroll=4)

    for n1 in range(PHASES):
        for r in range(ROWS):
            both = jnp.concatenate(
                [segments[2 * n1 + h, pl.ds(r * (NWIN + 1), NWIN), :] for h in range(2)], axis=1
            )
            samples[n1, pl.ds(r * NWIN, NWIN), :] = both.astype(jnp.bfloat16)
    for n1 in range(0, PHASES, 4):
        left = samples[n1 : n1 + 4].reshape(4 * SEGS, 2 * LANES)
        product = jnp.dot(left, high_ref[...], preferred_element_type=jnp.float32)
        product = product + jnp.dot(left, low_ref[...], preferred_element_type=jnp.float32)
        factor[n1 : n1 + 4] = product.reshape(4, SEGS, 2 * LANES)
    left = jnp.concatenate([samples[n1] for n1 in range(PHASES)], axis=1)
    middles[...] = jnp.dot(
        left, middle_ref[...].reshape(WIN, LANES), preferred_element_type=jnp.float32
    )

    zero_pair = jnp.zeros((SEGS, LANES), jnp.bfloat16)
    power[:, pl.ds(0, LANES)] = zero_pair
    power[:, pl.ds((2 * GROUPS + 1) * LANES, LANES)] = zero_pair

    def combine(pair, carry):
        powers = []
        for part in range(2):
            rows = pl.ds(pl.multiple_of(pair * 16 + part * ROWS, ROWS), ROWS)
            values = []
            for n1 in range(PHASES):
                re, im = factor[n1, rows, pl.ds(0, LANES)], factor[n1, rows, pl.ds(LANES, LANES)]
                if n1:
                    cos, sin = twiddle_ref[2 * n1], twiddle_ref[2 * n1 + 1]
                    re, im = re * cos + im * sin, im * cos - re * sin
                values.append((re, im))
            values = dft16(values)
            centre = middles[rows, :]
            centre = centre + roll_lanes(centre, -16)
            squares = []
            for g in range(GROUPS):
                for side in range(2):
                    re, im = values[15 - g] if side else values[g]
                    if side:
                        re = jnp.where(lane == 0, roll_lanes(centre, -g), re)
                        im = jnp.where(lane == 0, roll_lanes(centre, -(GROUPS + g)), im)
                    spectrum[4 * g + 2 * side, rows, :] = re
                    spectrum[4 * g + 2 * side + 1, rows, :] = im
                    squares.append(re * re + im * im)
            powers.append(squares)
        both = pl.ds(pl.multiple_of(pair * 16, 16), 16)
        for tile in range(2 * GROUPS):
            joined = jnp.concatenate([powers[0][tile], powers[1][tile]], axis=0)
            power[both, pl.ds((tile + 1) * LANES, LANES)] = joined.astype(jnp.bfloat16)
        return carry

    lax.fori_loop(0, SEGS // 16, combine, 0, unroll=4)

    for g in range(GROUPS):
        smooth[g] = jnp.dot(
            power[:, g * 256 : g * 256 + 512], box_ref[...], preferred_element_type=jnp.float32
        )
        for side in range(2):
            inverse = inverse_ref[2 * g + side]
            for c in range(2):
                sums = None
                for octet in range(NWIN // 8):
                    white = []
                    for o in range(NOFF):
                        rows = pl.ds((2 * o + c) * NWIN + octet * 8, 8)
                        level = smooth[g, rows, pl.ds(side * LANES, LANES)] * inverse
                        scale = lax.rsqrt(level + epsilon)
                        re = spectrum[4 * g + 2 * side, rows, :] * scale
                        im = spectrum[4 * g + 2 * side + 1, rows, :] * scale
                        white.append((re, im))
                    own_re, own_im = white[0]
                    terms = [own_re * own_re + own_im * own_im]
                    for far_re, far_im in white[1:]:
                        terms.append(own_re * far_re + own_im * far_im)
                        if side:
                            terms.append(own_re * far_im - own_im * far_re)
                        else:
                            terms.append(own_im * far_re - own_re * far_im)
                    sums = terms if sums is None else [a + b for a, b in zip(sums, terms)]
                place = (2 * g + side) * 2 + c
                rows = [sums[0], sums[1], sums[3], sums[5], zero, sums[2], sums[4], sums[6]]
                for index, value in enumerate(rows):
                    turned[place, pl.ds(index, 8, stride=9), :] = value
                result = [turned[place, pl.ds(9 * index, 8), :] for index in range(8)]
                result = functools.reduce(lambda a, b: a + b, result) * (1.0 / NWIN)
                if side:
                    folded[pl.ds((g * 2 + c) * 8, 8), :] = result
                else:
                    out_ref[c, :, pl.ds(g * 256, LANES)] = result[:NOFF]
                    out_ref[c, :, pl.ds(NF + g * 256, LANES)] = result[NOFF:]
    folded[...] = jnp.dot(
        folded[...],
        flip_ref[...],
        preferred_element_type=jnp.float32,
        precision=lax.Precision.HIGHEST,
    )
    for g in range(GROUPS):
        for c in range(2):
            row = (g * 2 + c) * 8
            out_ref[c, :, pl.ds(g * 256 + LANES, LANES)] = folded[pl.ds(row, 4), :]
            out_ref[c, :, pl.ds(NF + g * 256 + LANES, LANES)] = folded[pl.ds(row + 4, 4), :]


def stack(parts, starts):
    shards = parts.shape[0]
    vmem = pl.BlockSpec(memory_space=pltpu.VMEM)
    f32 = jnp.float32
    return pl.pallas_call(
        stack_kernel,
        out_shape=jax.ShapeDtypeStruct((2, NOFF, 2 * NF), f32),
        in_specs=[pl.BlockSpec(memory_space=pltpu.SMEM)] + [vmem] * 9,
        out_specs=vmem,
        scratch_shapes=[
            pltpu.VMEM((shards, ROWS * PITCH, LANES), f32),
            pltpu.VMEM((shards + 2, PHASES * ROWS, LANES), jnp.bfloat16),
            pltpu.VMEM((shards + 1, PHASES * ROWS, 2 * LANES), f32),
            pltpu.VMEM((PHASES, shards + 2, ROWS, LANES), f32),
            pltpu.VMEM((2 * PHASES, ROWS * (NWIN + 1), LANES), f32),
            pltpu.VMEM((PHASES, SEGS, 2 * LANES), jnp.bfloat16),
            pltpu.VMEM((PHASES, SEGS, 2 * LANES), f32),
            pltpu.VMEM((SEGS, LANES), f32),
            pltpu.VMEM((4 * GROUPS, SEGS, LANES), f32),
            pltpu.VMEM((SEGS, (2 * GROUPS + 2) * LANES), jnp.bfloat16),
            pltpu.VMEM((GROUPS, SEGS, 2 * LANES), f32),
            pltpu.VMEM((2 * GROUPS * 8, LANES), f32),
            pltpu.VMEM((4 * GROUPS, 72, LANES), f32),
        ],
        compiler_params=pltpu.CompilerParams(vmem_limit_bytes=40 * 1024 * 1024),
    )(starts, parts, *[jnp.asarray(table) for table in tables()])


def gather_kernel(offsets_ref, *refs):
    blocks, out_ref, nearby = refs[:-2], refs[-2], refs[-1]
    rows = blocks[0].shape[0]
    for index, block in enumerate(blocks):
        nearby[pl.ds(index * rows, rows)] = block[...]
    pair = ROWS // NOFF
    for o in range(NOFF):
        offset = offsets_ref[o]
        for member in range(out_ref.shape[0]):
            part = nearby[pl.ds(offset + pair * member, pair)]
            out_ref[member, pl.ds(pair * o, pair)] = part


def gather(blocks, offsets, members):
    rows = blocks[0].shape[0]
    vmem = pl.BlockSpec(memory_space=pltpu.VMEM)
    return pl.pallas_call(
        gather_kernel,
        out_shape=jax.ShapeDtypeStruct((members, ROWS, PHASES, LANES), jnp.bfloat16),
        in_specs=[pl.BlockSpec(memory_space=pltpu.SMEM)] + [vmem] * len(blocks),
        out_specs=vmem,
        scratch_shapes=[pltpu.VMEM((len(blocks) * rows, PHASES, LANES), jnp.bfloat16)],
        compiler_params=pltpu.CompilerParams(vmem_limit_bytes=16 * 1024 * 1024),
    )(offsets, *blocks)


def ahead_on(array, axis, by):
    size = lax.axis_size(axis)
    return lax.ppermute(array, axis, [((i + by) % size, i) for i in range(size)])


def body(records, dead_flags, starts, offsets):
    rows = records.shape[0]
    dealt = deal(records, dead_flags)
    reach = lax.axis_size("loop") // 2
    blocks = [dealt] + [ahead_on(dealt, "loop", by) for by in range(1, reach + 1)]
    outgoing = gather(blocks, offsets, lax.axis_size("chan"))
    parts = lax.all_to_all(outgoing, "chan", split_axis=0, concat_axis=0, tiled=True)
    return stack(parts, starts)


def solution(mesh):
    in_specs = (P("loop", "chan"), P("loop"), P(), P())
    out_specs = P(("loop", "chan"), None, None)
    return jax.shard_map(body, mesh=mesh, in_specs=in_specs, out_specs=out_specs, check_vma=False)
```

```python
import functools
import math

import jax
import jax.numpy as jnp
import ml_dtypes
import numpy as np
from jax import lax
from jax.experimental import pallas as pl
from jax.experimental.pallas import tpu as pltpu
from jax.sharding import PartitionSpec as P

NT = 32768
NF = 2048
NWIN = 32
NOFF = 4
RMW = 256
WB = 128
WIN = 4096
LANES = 128
PHASES = 16
PITCH = PHASES + 1
ROWS = 8
SEGS = ROWS * NWIN
GROUPS = NF // 256

epsilon = 1e-06


def split_table(table):
    high = table.astype(ml_dtypes.bfloat16)
    low = (table - high.astype(np.float64)).astype(ml_dtypes.bfloat16)
    return high, low


@functools.lru_cache(maxsize=None)
def tables():
    n2 = np.arange(256)[:, None]
    f2 = np.arange(LANES)[None, :]
    angle = 2.0 * math.pi * ((n2 * f2) % 256) / 256.0
    first = np.concatenate([np.cos(angle), -np.sin(angle)], axis=1)
    first_high, first_low = split_table(first)

    n1 = np.arange(PHASES)[:, None]
    angle = 2.0 * math.pi * ((n1 * f2) % WIN) / WIN
    twiddle = np.stack([np.cos(angle), np.sin(angle)], axis=1)
    twiddle = np.broadcast_to(twiddle[:, :, None, :], (PHASES, 2, ROWS, LANES))
    twiddle = np.ascontiguousarray(twiddle.reshape(2 * PHASES, ROWS, LANES)).astype(np.float32)

    sample = (np.arange(PHASES)[:, None] + PHASES * np.arange(256)[None, :])[:, :, None]
    group = np.arange(GROUPS)[None, None, :]
    angle = 2.0 * math.pi * (((1 + 2 * group) * sample) % 32) / 32.0
    middle = np.concatenate([np.cos(angle), np.sin(angle)], axis=2)
    high, low = split_table(middle)
    middle = np.zeros((PHASES, 256, LANES), ml_dtypes.bfloat16)
    middle[:, :, :16] = high
    middle[:, :, 16:32] = low

    lane = np.arange(LANES)
    upper = np.where(lane == 0, 128, 256 - lane)
    rows = np.concatenate([upper - 256, lane, upper, lane + 256])[:, None]
    columns = np.concatenate([lane, upper])[None, :]
    box = ((rows >= columns - WB // 2) & (rows < columns + WB // 2)).astype(ml_dtypes.bfloat16)

    bins = np.arange(GROUPS)[:, None] * 256 + np.concatenate([lane, upper])[None, :]
    count = np.minimum(bins + WB // 2, NF) - np.maximum(bins - WB // 2, 0)
    inverse = (1.0 / count).astype(np.float32).reshape(2 * GROUPS, 1, LANES)
    inverse = np.ascontiguousarray(np.broadcast_to(inverse, (2 * GROUPS, ROWS, LANES)))

    flip = np.zeros((LANES, LANES), np.float32)
    flip[(LANES - lane) % LANES, lane] = 1.0
    row = np.arange(2 * LANES)[:, None]
    shift = np.concatenate([row == 120 + lane[None, :], row == 8 + lane[None, :]], axis=1)
    shift = shift.astype(ml_dtypes.bfloat16)
    return shift, first_high, first_low, twiddle, middle, box, inverse, flip


def lane_index(rows=ROWS):
    return lax.broadcasted_iota(jnp.int32, (rows, LANES), 1)


def roll_lanes(value, by):
    return pltpu.roll(value, by % LANES, 1)


def deal_kernel(records_ref, live_ref, out_ref, staged):
    rows = records_ref.shape[0]
    source = lax.broadcasted_iota(jnp.int32, (256, 256), 0)
    target = lax.broadcasted_iota(jnp.int32, (256, 256), 1)
    table = (source == (target % 16) * 16 + target // 16).astype(jnp.bfloat16)
    place = lax.broadcasted_iota(jnp.int32, (rows, rows), 0)
    across = lax.broadcasted_iota(jnp.int32, (rows, rows), 1)
    live = jnp.where(place == across, live_ref[...], 0.0)
    live = jnp.sum(live, axis=1, keepdims=True)
    lane = lane_index(rows)
    parts = [[None] * 8, [None] * 8]
    for chunk in range(8):
        product = jnp.dot(
            records_ref[:, chunk * 256 : (chunk + 1) * 256],
            table,
            preferred_element_type=jnp.float32,
        )
        parts[0][chunk] = product[:, :LANES]
        parts[1][chunk] = product[:, LANES:]
    for half in range(2):
        current = parts[half]
        for bit in (1, 2, 4):
            step = 16 * bit
            keep = (lane // step) % 2 == 0
            following = list(current)
            for index in range(8):
                if index & bit == 0:
                    low, high = current[index], current[index | bit]
                    following[index] = jnp.where(keep, low, roll_lanes(high, step))
                    following[index | bit] = jnp.where(keep, roll_lanes(low, -step), high)
            current = following
        for index in range(8):
            staged[pl.ds(half * 8 + index, rows, stride=PITCH), :] = current[index] * live
    for r in range(rows):
        out_ref[r] = staged[pl.ds(r * PITCH, PHASES), :].astype(jnp.bfloat16)


def deal(records, dead_flags):
    rows = records.shape[0]
    live = (1 - dead_flags).astype(jnp.float32).reshape(1, rows)
    vmem = pl.BlockSpec(memory_space=pltpu.VMEM)
    return pl.pallas_call(
        deal_kernel,
        out_shape=jax.ShapeDtypeStruct((rows, PHASES, LANES), jnp.bfloat16),
        in_specs=[vmem] * 2,
        out_specs=vmem,
        scratch_shapes=[pltpu.VMEM((rows * PITCH, LANES), jnp.float32)],
        compiler_params=pltpu.CompilerParams(vmem_limit_bytes=16 * 1024 * 1024),
    )(records, live)


def dft4(a, b, c, d):
    (ar, ai), (br, bi), (cr, ci), (dr, di) = a, b, c, d
    sr, si, tr, ti = ar + cr, ai + ci, ar - cr, ai - ci
    ur, ui, vr, vi = br + dr, bi + di, br - dr, bi - di
    return [(sr + ur, si + ui), (tr + vi, ti - vr), (sr - ur, si - ui), (tr - vi, ti + vr)]


def rotate(value, power):
    re, im = value
    power %= 16
    if power == 0:
        return value
    if power == 4:
        return (im, -re)
    root = math.sqrt(0.5)
    if power == 2:
        return ((re + im) * root, (im - re) * root)
    if power == 6:
        return ((im - re) * root, (re + im) * (-root))
    cos, sin = math.cos(2 * math.pi * power / 16), math.sin(2 * math.pi * power / 16)
    return (re * cos + im * sin, im * cos - re * sin)


def dft16(values):
    inner = [dft4(values[q], values[q + 4], values[q + 8], values[q + 12]) for q in range(4)]
    result = [None] * 16
    for k in range(4):
        outer = dft4(*[rotate(inner[q][k], q * k) for q in range(4)])
        for j in range(4):
            result[k + 4 * j] = outer[j]
    return result


def stack_kernel(
    starts_ref,
    parts_ref,
    shift_ref,
    high_ref,
    low_ref,
    twiddle_ref,
    middle_ref,
    box_ref,
    inverse_ref,
    flip_ref,
    out_ref,
    plain,
    levels,
    moved,
    normed,
    segments,
    samples,
    factor,
    middles,
    spectrum,
    power,
    smooth,
    folded,
    turned,
):
    lane = lane_index()
    shards = parts_ref.shape[0]
    for k in range(shards):
        for r in range(ROWS):
            plain[k, pl.ds(r * PITCH, PHASES), :] = parts_ref[k, r].astype(jnp.float32)

    none = jnp.zeros((PHASES * ROWS, LANES), jnp.bfloat16)
    levels[0] = none
    levels[shards + 1] = none
    totals = []
    for k in range(shards):
        level = [jnp.abs(plain[k, pl.ds(p, ROWS, stride=PITCH), :]) for p in range(PHASES)]
        totals.append(functools.reduce(lambda a, b: a + b, level))
        levels[k + 1] = jnp.concatenate(level, axis=0).astype(jnp.bfloat16)
    pairs = jnp.concatenate([levels[: shards + 1], levels[1:]], axis=2)
    pairs = pairs.reshape((shards + 1) * PHASES * ROWS, 2 * LANES)
    product = jnp.dot(pairs, shift_ref[...], preferred_element_type=jnp.float32)
    moved[...] = product.reshape(shards + 1, PHASES * ROWS, 2 * LANES)
    zero = jnp.zeros((ROWS, LANES), jnp.float32)

    def ahead(tiles, by):
        rolled = [roll_lanes(tile, -by) for tile in tiles] + [zero]
        return [jnp.where(lane < LANES - by, rolled[k], rolled[k + 1]) for k in range(len(tiles))]

    def behind(tiles, by):
        rolled = [zero] + [roll_lanes(tile, by) for tile in tiles]
        return [jnp.where(lane >= by, rolled[k + 1], rolled[k]) for k in range(len(tiles))]

    def plus(*lists):
        return [functools.reduce(lambda a, b: a + b, group) for group in zip(*lists)]

    two = plus(totals, ahead(totals, 1))
    four = plus(two, ahead(two, 2))
    columns = plus(ahead(four, 1), ahead(two, 5), ahead(totals, 7))
    past = totals
    for by in (1, 2, 4):
        past = plus(past, behind(past, by))
    columns = plus(columns, past)
    for k in range(shards):
        running = zero
        after = [None] * PHASES
        for p in reversed(range(PHASES)):
            running = running + moved[k, pl.ds(p * ROWS, ROWS), pl.ds(0, LANES)]
            after[p] = running
        running = columns[k]
        for p in range(PHASES):
            total = running + after[p]
            running = running + moved[k + 1, pl.ds(p * ROWS, ROWS), pl.ds(LANES, LANES)]
            if k in (0, shards - 1):
                place = p + PHASES * (k * LANES + lane)
                count = jnp.minimum(place + RMW // 2, NT) - jnp.maximum(place - RMW // 2, 0)
                mean_level = total / count.astype(jnp.float32)
            else:
                mean_level = total * (1.0 / RMW)
            signal = plain[k, pl.ds(p, ROWS, stride=PITCH), :]
            ratio = signal / (mean_level + epsilon)
            normed[p, k] = ratio.astype(jnp.bfloat16).astype(jnp.float32)

    place = lane * PHASES

    def cut(w, carry):
        start = starts_ref[w]
        tile = (start >> 12) * 2
        first = start & (WIN - 1)
        for p in range(PHASES):
            for half in range(2):
                keep = place >= first - (half * LANES * PHASES + p)
                joined = jnp.where(keep, normed[p, tile + half], normed[p, tile + 2 + half])
                segments[2 * p + half, pl.ds(w, ROWS, stride=NWIN + 1), :] = joined
        return carry

    lax.fori_loop(0, NWIN, cut, 0, unroll=4)

    for n1 in range(PHASES):
        for r in range(ROWS):
            both = jnp.concatenate(
                [segments[2 * n1 + h, pl.ds(r * (NWIN + 1), NWIN), :] for h in range(2)], axis=1
            )
            samples[n1, pl.ds(r * NWIN, NWIN), :] = both.astype(jnp.bfloat16)
    for n1 in range(0, PHASES, 4):
        left = samples[n1 : n1 + 4].reshape(4 * SEGS, 2 * LANES)
        product = jnp.dot(left, high_ref[...], preferred_element_type=jnp.float32)
        product = product + jnp.dot(left, low_ref[...], preferred_element_type=jnp.float32)
        factor[n1 : n1 + 4] = product.reshape(4, SEGS, 2 * LANES)
    left = jnp.concatenate([samples[n1] for n1 in range(PHASES)], axis=1)
    middles[...] = jnp.dot(
        left, middle_ref[...].reshape(WIN, LANES), preferred_element_type=jnp.float32
    )

    zero_pair = jnp.zeros((SEGS, LANES), jnp.bfloat16)
    power[:, pl.ds(0, LANES)] = zero_pair
    power[:, pl.ds((2 * GROUPS + 1) * LANES, LANES)] = zero_pair

    def combine(pair, carry):
        powers = []
        for part in range(2):
            rows = pl.ds(pl.multiple_of(pair * 16 + part * ROWS, ROWS), ROWS)
            values = []
            for n1 in range(PHASES):
                re, im = factor[n1, rows, pl.ds(0, LANES)], factor[n1, rows, pl.ds(LANES, LANES)]
                if n1:
                    cos, sin = twiddle_ref[2 * n1], twiddle_ref[2 * n1 + 1]
                    re, im = re * cos + im * sin, im * cos - re * sin
                values.append((re, im))
            values = dft16(values)
            centre = middles[rows, :]
            centre = centre + roll_lanes(centre, -16)
            squares = []
            for g in range(GROUPS):
                for side in range(2):
                    re, im = values[15 - g] if side else values[g]
                    if side:
                        re = jnp.where(lane == 0, roll_lanes(centre, -g), re)
                        im = jnp.where(lane == 0, roll_lanes(centre, -(GROUPS + g)), im)
                    spectrum[4 * g + 2 * side, rows, :] = re
                    spectrum[4 * g + 2 * side + 1, rows, :] = im
                    squares.append(re * re + im * im)
            powers.append(squares)
        both = pl.ds(pl.multiple_of(pair * 16, 16), 16)
        for tile in range(2 * GROUPS):
            joined = jnp.concatenate([powers[0][tile], powers[1][tile]], axis=0)
            power[both, pl.ds((tile + 1) * LANES, LANES)] = joined.astype(jnp.bfloat16)
        return carry

    lax.fori_loop(0, SEGS // 16, combine, 0, unroll=4)

    for g in range(GROUPS):
        smooth[g] = jnp.dot(
            power[:, g * 256 : g * 256 + 512], box_ref[...], preferred_element_type=jnp.float32
        )
        for side in range(2):
            inverse = inverse_ref[2 * g + side]
            for c in range(2):
                sums = None
                for octet in range(NWIN // 8):
                    white = []
                    for o in range(NOFF):
                        rows = pl.ds((2 * o + c) * NWIN + octet * 8, 8)
                        level = smooth[g, rows, pl.ds(side * LANES, LANES)] * inverse
                        scale = lax.rsqrt(level + epsilon)
                        re = spectrum[4 * g + 2 * side, rows, :] * scale
                        im = spectrum[4 * g + 2 * side + 1, rows, :] * scale
                        white.append((re, im))
                    own_re, own_im = white[0]
                    terms = [own_re * own_re + own_im * own_im]
                    for far_re, far_im in white[1:]:
                        terms.append(own_re * far_re + own_im * far_im)
                        if side:
                            terms.append(own_re * far_im - own_im * far_re)
                        else:
                            terms.append(own_im * far_re - own_re * far_im)
                    sums = terms if sums is None else [a + b for a, b in zip(sums, terms)]
                place = (2 * g + side) * 2 + c
                rows = [sums[0], sums[1], sums[3], sums[5], zero, sums[2], sums[4], sums[6]]
                for index, value in enumerate(rows):
                    turned[place, pl.ds(index, 8, stride=9), :] = value
                result = [turned[place, pl.ds(9 * index, 8), :] for index in range(8)]
                result = functools.reduce(lambda a, b: a + b, result) * (1.0 / NWIN)
                if side:
                    folded[pl.ds((g * 2 + c) * 8, 8), :] = result
                else:
                    out_ref[c, :, pl.ds(g * 256, LANES)] = result[:NOFF]
                    out_ref[c, :, pl.ds(NF + g * 256, LANES)] = result[NOFF:]
    folded[...] = jnp.dot(
        folded[...],
        flip_ref[...],
        preferred_element_type=jnp.float32,
        precision=lax.Precision.HIGHEST,
    )
    for g in range(GROUPS):
        for c in range(2):
            row = (g * 2 + c) * 8
            out_ref[c, :, pl.ds(g * 256 + LANES, LANES)] = folded[pl.ds(row, 4), :]
            out_ref[c, :, pl.ds(NF + g * 256 + LANES, LANES)] = folded[pl.ds(row + 4, 4), :]


def stack(parts, starts):
    shards = parts.shape[0]
    vmem = pl.BlockSpec(memory_space=pltpu.VMEM)
    f32 = jnp.float32
    return pl.pallas_call(
        stack_kernel,
        out_shape=jax.ShapeDtypeStruct((2, NOFF, 2 * NF), f32),
        in_specs=[pl.BlockSpec(memory_space=pltpu.SMEM)] + [vmem] * 9,
        out_specs=vmem,
        scratch_shapes=[
            pltpu.VMEM((shards, ROWS * PITCH, LANES), f32),
            pltpu.VMEM((shards + 2, PHASES * ROWS, LANES), jnp.bfloat16),
            pltpu.VMEM((shards + 1, PHASES * ROWS, 2 * LANES), f32),
            pltpu.VMEM((PHASES, shards + 2, ROWS, LANES), f32),
            pltpu.VMEM((2 * PHASES, ROWS * (NWIN + 1), LANES), f32),
            pltpu.VMEM((PHASES, SEGS, 2 * LANES), jnp.bfloat16),
            pltpu.VMEM((PHASES, SEGS, 2 * LANES), f32),
            pltpu.VMEM((SEGS, LANES), f32),
            pltpu.VMEM((4 * GROUPS, SEGS, LANES), f32),
            pltpu.VMEM((SEGS, (2 * GROUPS + 2) * LANES), jnp.bfloat16),
            pltpu.VMEM((GROUPS, SEGS, 2 * LANES), f32),
            pltpu.VMEM((2 * GROUPS * 8, LANES), f32),
            pltpu.VMEM((4 * GROUPS, 72, LANES), f32),
        ],
        compiler_params=pltpu.CompilerParams(vmem_limit_bytes=40 * 1024 * 1024),
    )(starts, parts, *[jnp.asarray(table) for table in tables()])


ORDER = (0, 1, 2, 4, 3)


def gather_kernel(offsets_ref, *refs):
    blocks, out_ref, nearby = refs[:-2], refs[-2], refs[-1]
    rows = blocks[0].shape[0]
    for index, block in zip(ORDER, blocks):
        nearby[pl.ds(index * rows, rows)] = block[...]
    pair = ROWS // NOFF
    for o in range(NOFF):
        offset = offsets_ref[o]
        for member in range(out_ref.shape[0]):
            part = nearby[pl.ds(offset + pair * member, pair)]
            out_ref[member, pl.ds(pair * o, pair)] = part


def gather(blocks, offsets, members):
    rows = blocks[0].shape[0]
    vmem = pl.BlockSpec(memory_space=pltpu.VMEM)
    return pl.pallas_call(
        gather_kernel,
        out_shape=jax.ShapeDtypeStruct((members, ROWS, PHASES, LANES), jnp.bfloat16),
        in_specs=[pl.BlockSpec(memory_space=pltpu.SMEM)] + [vmem] * len(blocks),
        out_specs=vmem,
        scratch_shapes=[pltpu.VMEM((len(blocks) * rows, PHASES, LANES), jnp.bfloat16)],
        compiler_params=pltpu.CompilerParams(vmem_limit_bytes=16 * 1024 * 1024),
    )(offsets, *[blocks[index] for index in ORDER])


def ahead_on(array, axis, by):
    size = lax.axis_size(axis)
    return lax.ppermute(array, axis, [((i + by) % size, i) for i in range(size)])


def body(records, dead_flags, starts, offsets):
    rows = records.shape[0]
    dealt = deal(records, dead_flags)
    reach = lax.axis_size("loop") // 2
    blocks = [dealt] + [ahead_on(dealt, "loop", by) for by in range(1, reach + 1)]
    outgoing = gather(blocks, offsets, lax.axis_size("chan"))
    parts = lax.all_to_all(outgoing, "chan", split_axis=0, concat_axis=0, tiled=True)
    return stack(parts, starts)


def solution(mesh):
    in_specs = (P("loop", "chan"), P("loop"), P(), P())
    out_specs = P(("loop", "chan"), None, None)
    return jax.shard_map(body, mesh=mesh, in_specs=in_specs, out_specs=out_specs, check_vma=False)
```

```python
import functools
import math

import jax
import jax.numpy as jnp
import ml_dtypes
import numpy as np
from jax import lax
from jax.experimental import pallas as pl
from jax.experimental.pallas import tpu as pltpu
from jax.sharding import PartitionSpec as P

NT = 32768
NF = 2048
NWIN = 32
NOFF = 4
RMW = 256
WB = 128
WIN = 4096
LANES = 128
PHASES = 16
PITCH = PHASES + 1
ROWS = 8
SEGS = ROWS * NWIN
GROUPS = NF // 256

epsilon = 1e-06


def split_table(table):
    high = table.astype(ml_dtypes.bfloat16)
    low = (table - high.astype(np.float64)).astype(ml_dtypes.bfloat16)
    return high, low


@functools.lru_cache(maxsize=None)
def tables():
    n2 = np.arange(256)[:, None]
    f2 = np.arange(LANES)[None, :]
    angle = 2.0 * math.pi * ((n2 * f2) % 256) / 256.0
    first = np.concatenate([np.cos(angle), -np.sin(angle)], axis=1)
    first_high, first_low = split_table(first)

    n1 = np.arange(PHASES)[:, None]
    angle = 2.0 * math.pi * ((n1 * f2) % WIN) / WIN
    twiddle = np.stack([np.cos(angle), np.sin(angle)], axis=1)
    twiddle = np.broadcast_to(twiddle[:, :, None, :], (PHASES, 2, ROWS, LANES))
    twiddle = np.ascontiguousarray(twiddle.reshape(2 * PHASES, ROWS, LANES)).astype(np.float32)

    sample = (np.arange(PHASES)[:, None] + PHASES * np.arange(256)[None, :])[:, :, None]
    group = np.arange(GROUPS)[None, None, :]
    angle = 2.0 * math.pi * (((1 + 2 * group) * sample) % 32) / 32.0
    middle = np.concatenate([np.cos(angle), np.sin(angle)], axis=2)
    high, low = split_table(middle)
    middle = np.zeros((PHASES, 256, LANES), ml_dtypes.bfloat16)
    middle[:, :, :16] = high
    middle[:, :, 16:32] = low

    lane = np.arange(LANES)
    upper = np.where(lane == 0, 128, 256 - lane)
    rows = np.concatenate([upper - 256, lane, upper, lane + 256])[:, None]
    columns = np.concatenate([lane, upper])[None, :]
    box = ((rows >= columns - WB // 2) & (rows < columns + WB // 2)).astype(ml_dtypes.bfloat16)

    bins = np.arange(GROUPS)[:, None] * 256 + np.concatenate([lane, upper])[None, :]
    count = np.minimum(bins + WB // 2, NF) - np.maximum(bins - WB // 2, 0)
    inverse = (1.0 / count).astype(np.float32).reshape(2 * GROUPS, 1, LANES)
    inverse = np.ascontiguousarray(np.broadcast_to(inverse, (2 * GROUPS, ROWS, LANES)))

    flip = np.zeros((LANES, LANES), np.float32)
    flip[(LANES - lane) % LANES, lane] = 1.0
    row = np.arange(2 * LANES)[:, None]
    shift = np.concatenate([row == 120 + lane[None, :], row == 8 + lane[None, :]], axis=1)
    shift = shift.astype(ml_dtypes.bfloat16)
    return shift, first_high, first_low, twiddle, middle, box, inverse, flip


def lane_index(rows=ROWS):
    return lax.broadcasted_iota(jnp.int32, (rows, LANES), 1)


def roll_lanes(value, by):
    return pltpu.roll(value, by % LANES, 1)


def deal_kernel(records_ref, live_ref, out_ref, staged):
    rows = records_ref.shape[0]
    source = lax.broadcasted_iota(jnp.int32, (256, 256), 0)
    target = lax.broadcasted_iota(jnp.int32, (256, 256), 1)
    table = (source == (target % 16) * 16 + target // 16).astype(jnp.bfloat16)
    place = lax.broadcasted_iota(jnp.int32, (rows, rows), 0)
    across = lax.broadcasted_iota(jnp.int32, (rows, rows), 1)
    live = jnp.where(place == across, live_ref[...], 0.0)
    live = jnp.sum(live, axis=1, keepdims=True)
    lane = lane_index(rows)
    parts = [[None] * 8, [None] * 8]
    for chunk in range(8):
        product = jnp.dot(
            records_ref[:, chunk * 256 : (chunk + 1) * 256],
            table,
            preferred_element_type=jnp.float32,
        )
        parts[0][chunk] = product[:, :LANES]
        parts[1][chunk] = product[:, LANES:]
    for half in range(2):
        current = parts[half]
        for bit in (1, 2, 4):
            step = 16 * bit
            keep = (lane // step) % 2 == 0
            following = list(current)
            for index in range(8):
                if index & bit == 0:
                    low, high = current[index], current[index | bit]
                    following[index] = jnp.where(keep, low, roll_lanes(high, step))
                    following[index | bit] = jnp.where(keep, roll_lanes(low, -step), high)
            current = following
        for index in range(8):
            staged[pl.ds(half * 8 + index, rows, stride=PITCH), :] = current[index] * live
    for r in range(rows):
        out_ref[r] = staged[pl.ds(r * PITCH, PHASES), :].astype(jnp.bfloat16)


def deal(records, dead_flags):
    rows = records.shape[0]
    live = (1 - dead_flags).astype(jnp.float32).reshape(1, rows)
    vmem = pl.BlockSpec(memory_space=pltpu.VMEM)
    return pl.pallas_call(
        deal_kernel,
        out_shape=jax.ShapeDtypeStruct((rows, PHASES, LANES), jnp.bfloat16),
        in_specs=[vmem] * 2,
        out_specs=vmem,
        scratch_shapes=[pltpu.VMEM(((rows + 1) * PITCH - 1, LANES), jnp.float32)],
        compiler_params=pltpu.CompilerParams(vmem_limit_bytes=16 * 1024 * 1024),
    )(records, live)


def dft4(a, b, c, d):
    (ar, ai), (br, bi), (cr, ci), (dr, di) = a, b, c, d
    sr, si, tr, ti = ar + cr, ai + ci, ar - cr, ai - ci
    ur, ui, vr, vi = br + dr, bi + di, br - dr, bi - di
    return [(sr + ur, si + ui), (tr + vi, ti - vr), (sr - ur, si - ui), (tr - vi, ti + vr)]


def rotate(value, power):
    re, im = value
    power %= 16
    if power == 0:
        return value
    if power == 4:
        return (im, -re)
    root = math.sqrt(0.5)
    if power == 2:
        return ((re + im) * root, (im - re) * root)
    if power == 6:
        return ((im - re) * root, (re + im) * (-root))
    cos, sin = math.cos(2 * math.pi * power / 16), math.sin(2 * math.pi * power / 16)
    return (re * cos + im * sin, im * cos - re * sin)


def dft16(values):
    inner = [dft4(values[q], values[q + 4], values[q + 8], values[q + 12]) for q in range(4)]
    result = [None] * 16
    for k in range(4):
        outer = dft4(*[rotate(inner[q][k], q * k) for q in range(4)])
        for j in range(4):
            result[k + 4 * j] = outer[j]
    return result


def stack_kernel(
    starts_ref,
    parts_ref,
    shift_ref,
    high_ref,
    low_ref,
    twiddle_ref,
    middle_ref,
    box_ref,
    inverse_ref,
    flip_ref,
    out_ref,
    plain,
    levels,
    moved,
    normed,
    segments,
    samples,
    factor,
    middles,
    spectrum,
    power,
    smooth,
    folded,
    turned,
):
    lane = lane_index()
    shards = parts_ref.shape[0]
    for k in range(shards):
        for r in range(ROWS):
            plain[k, pl.ds(r * PITCH, PHASES), :] = parts_ref[k, r].astype(jnp.float32)

    none = jnp.zeros((PHASES * ROWS, LANES), jnp.bfloat16)
    levels[0] = none
    levels[shards + 1] = none
    totals = []
    for k in range(shards):
        level = [jnp.abs(plain[k, pl.ds(p, ROWS, stride=PITCH), :]) for p in range(PHASES)]
        totals.append(functools.reduce(lambda a, b: a + b, level))
        levels[k + 1] = jnp.concatenate(level, axis=0).astype(jnp.bfloat16)
    pairs = jnp.concatenate([levels[: shards + 1], levels[1:]], axis=2)
    pairs = pairs.reshape((shards + 1) * PHASES * ROWS, 2 * LANES)
    product = jnp.dot(pairs, shift_ref[...], preferred_element_type=jnp.float32)
    moved[...] = product.reshape(shards + 1, PHASES * ROWS, 2 * LANES)
    zero = jnp.zeros((ROWS, LANES), jnp.float32)

    def ahead(tiles, by):
        rolled = [roll_lanes(tile, -by) for tile in tiles] + [zero]
        return [jnp.where(lane < LANES - by, rolled[k], rolled[k + 1]) for k in range(len(tiles))]

    def behind(tiles, by):
        rolled = [zero] + [roll_lanes(tile, by) for tile in tiles]
        return [jnp.where(lane >= by, rolled[k + 1], rolled[k]) for k in range(len(tiles))]

    def plus(*lists):
        return [functools.reduce(lambda a, b: a + b, group) for group in zip(*lists)]

    two = plus(totals, ahead(totals, 1))
    four = plus(two, ahead(two, 2))
    columns = plus(ahead(four, 1), ahead(two, 5), ahead(totals, 7))
    past = totals
    for by in (1, 2, 4):
        past = plus(past, behind(past, by))
    columns = plus(columns, past)
    for k in range(shards):
        running = zero
        after = [None] * PHASES
        for p in reversed(range(PHASES)):
            running = running + moved[k, pl.ds(p * ROWS, ROWS), pl.ds(0, LANES)]
            after[p] = running
        running = columns[k]
        for p in range(PHASES):
            total = running + after[p]
            running = running + moved[k + 1, pl.ds(p * ROWS, ROWS), pl.ds(LANES, LANES)]
            if k in (0, shards - 1):
                place = p + PHASES * (k * LANES + lane)
                count = jnp.minimum(place + RMW // 2, NT) - jnp.maximum(place - RMW // 2, 0)
                mean_level = total / count.astype(jnp.float32)
            else:
                mean_level = total * (1.0 / RMW)
            signal = plain[k, pl.ds(p, ROWS, stride=PITCH), :]
            ratio = signal / (mean_level + epsilon)
            normed[p, k] = ratio.astype(jnp.bfloat16).astype(jnp.float32)

    place = lane * PHASES

    def cut(w, carry):
        start = starts_ref[w]
        tile = (start >> 12) * 2
        first = start & (WIN - 1)
        for p in range(PHASES):
            for half in range(2):
                keep = place >= first - (half * LANES * PHASES + p)
                joined = jnp.where(keep, normed[p, tile + half], normed[p, tile + 2 + half])
                segments[2 * p + half, pl.ds(w, ROWS, stride=NWIN + 1), :] = joined
        return carry

    lax.fori_loop(0, NWIN, cut, 0, unroll=4)

    for n1 in range(PHASES):
        for r in range(ROWS):
            both = jnp.concatenate(
                [segments[2 * n1 + h, pl.ds(r * (NWIN + 1), NWIN), :] for h in range(2)], axis=1
            )
            samples[n1, pl.ds(r * NWIN, NWIN), :] = both.astype(jnp.bfloat16)
    for n1 in range(0, PHASES, 4):
        left = samples[n1 : n1 + 4].reshape(4 * SEGS, 2 * LANES)
        product = jnp.dot(left, high_ref[...], preferred_element_type=jnp.float32)
        product = product + jnp.dot(left, low_ref[...], preferred_element_type=jnp.float32)
        factor[n1 : n1 + 4] = product.reshape(4, SEGS, 2 * LANES)
    left = jnp.concatenate([samples[n1] for n1 in range(PHASES)], axis=1)
    middles[...] = jnp.dot(
        left, middle_ref[...].reshape(WIN, LANES), preferred_element_type=jnp.float32
    )

    zero_pair = jnp.zeros((SEGS, LANES), jnp.bfloat16)
    power[:, pl.ds(0, LANES)] = zero_pair
    power[:, pl.ds((2 * GROUPS + 1) * LANES, LANES)] = zero_pair

    def combine(pair, carry):
        powers = []
        for part in range(2):
            rows = pl.ds(pl.multiple_of(pair * 16 + part * ROWS, ROWS), ROWS)
            values = []
            for n1 in range(PHASES):
                re, im = factor[n1, rows, pl.ds(0, LANES)], factor[n1, rows, pl.ds(LANES, LANES)]
                if n1:
                    cos, sin = twiddle_ref[2 * n1], twiddle_ref[2 * n1 + 1]
                    re, im = re * cos + im * sin, im * cos - re * sin
                values.append((re, im))
            values = dft16(values)
            centre = middles[rows, :]
            centre = centre + roll_lanes(centre, -16)
            squares = []
            for g in range(GROUPS):
                for side in range(2):
                    re, im = values[15 - g] if side else values[g]
                    if side:
                        re = jnp.where(lane == 0, roll_lanes(centre, -g), re)
                        im = jnp.where(lane == 0, roll_lanes(centre, -(GROUPS + g)), im)
                    spectrum[4 * g + 2 * side, rows, :] = re
                    spectrum[4 * g + 2 * side + 1, rows, :] = im
                    squares.append(re * re + im * im)
            powers.append(squares)
        both = pl.ds(pl.multiple_of(pair * 16, 16), 16)
        for tile in range(2 * GROUPS):
            joined = jnp.concatenate([powers[0][tile], powers[1][tile]], axis=0)
            power[both, pl.ds((tile + 1) * LANES, LANES)] = joined.astype(jnp.bfloat16)
        return carry

    lax.fori_loop(0, SEGS // 16, combine, 0, unroll=4)

    for g in range(GROUPS):
        smooth[g] = jnp.dot(
            power[:, g * 256 : g * 256 + 512], box_ref[...], preferred_element_type=jnp.float32
        )
        for side in range(2):
            inverse = inverse_ref[2 * g + side]
            for c in range(2):
                sums = None
                for octet in range(NWIN // 8):
                    white = []
                    for o in range(NOFF):
                        rows = pl.ds((2 * o + c) * NWIN + octet * 8, 8)
                        level = smooth[g, rows, pl.ds(side * LANES, LANES)] * inverse
                        scale = lax.rsqrt(level + epsilon)
                        re = spectrum[4 * g + 2 * side, rows, :] * scale
                        im = spectrum[4 * g + 2 * side + 1, rows, :] * scale
                        white.append((re, im))
                    own_re, own_im = white[0]
                    terms = [own_re * own_re + own_im * own_im]
                    for far_re, far_im in white[1:]:
                        terms.append(own_re * far_re + own_im * far_im)
                        if side:
                            terms.append(own_re * far_im - own_im * far_re)
                        else:
                            terms.append(own_im * far_re - own_re * far_im)
                    sums = terms if sums is None else [a + b for a, b in zip(sums, terms)]
                place = (2 * g + side) * 2 + c
                rows = [sums[0], sums[1], sums[3], sums[5], zero, sums[2], sums[4], sums[6]]
                for index, value in enumerate(rows):
                    turned[place, pl.ds(index, 8, stride=9), :] = value
                result = [turned[place, pl.ds(9 * index, 8), :] for index in range(8)]
                result = functools.reduce(lambda a, b: a + b, result) * (1.0 / NWIN)
                if side:
                    folded[pl.ds((g * 2 + c) * 8, 8), :] = result
                else:
                    out_ref[c, :, pl.ds(g * 256, LANES)] = result[:NOFF]
                    out_ref[c, :, pl.ds(NF + g * 256, LANES)] = result[NOFF:]
    folded[...] = jnp.dot(
        folded[...],
        flip_ref[...],
        preferred_element_type=jnp.float32,
        precision=lax.Precision.HIGHEST,
    )
    for g in range(GROUPS):
        for c in range(2):
            row = (g * 2 + c) * 8
            out_ref[c, :, pl.ds(g * 256 + LANES, LANES)] = folded[pl.ds(row, 4), :]
            out_ref[c, :, pl.ds(NF + g * 256 + LANES, LANES)] = folded[pl.ds(row + 4, 4), :]


def stack(parts, starts):
    shards = parts.shape[0]
    vmem = pl.BlockSpec(memory_space=pltpu.VMEM)
    f32 = jnp.float32
    return pl.pallas_call(
        stack_kernel,
        out_shape=jax.ShapeDtypeStruct((2, NOFF, 2 * NF), f32),
        in_specs=[pl.BlockSpec(memory_space=pltpu.SMEM)] + [vmem] * 9,
        out_specs=vmem,
        scratch_shapes=[
            pltpu.VMEM((shards, (ROWS + 1) * PITCH - 1, LANES), f32),
            pltpu.VMEM((shards + 2, PHASES * ROWS, LANES), jnp.bfloat16),
            pltpu.VMEM((shards + 1, PHASES * ROWS, 2 * LANES), f32),
            pltpu.VMEM((PHASES, shards + 2, ROWS, LANES), f32),
            pltpu.VMEM((2 * PHASES, (ROWS + 1) * (NWIN + 1) - 1, LANES), f32),
            pltpu.VMEM((PHASES, SEGS, 2 * LANES), jnp.bfloat16),
            pltpu.VMEM((PHASES, SEGS, 2 * LANES), f32),
            pltpu.VMEM((SEGS, LANES), f32),
            pltpu.VMEM((4 * GROUPS, SEGS, LANES), f32),
            pltpu.VMEM((SEGS, (2 * GROUPS + 2) * LANES), jnp.bfloat16),
            pltpu.VMEM((GROUPS, SEGS, 2 * LANES), f32),
            pltpu.VMEM((2 * GROUPS * 8, LANES), f32),
            pltpu.VMEM((4 * GROUPS, 80, LANES), f32),
        ],
        compiler_params=pltpu.CompilerParams(vmem_limit_bytes=40 * 1024 * 1024),
    )(starts, parts, *[jnp.asarray(table) for table in tables()])


ORDER = (0, 1, 2, 4, 3)


def gather_kernel(offsets_ref, *refs):
    blocks, out_ref, nearby = refs[:-2], refs[-2], refs[-1]
    rows = blocks[0].shape[0]
    for index, block in zip(ORDER, blocks):
        nearby[pl.ds(index * rows, rows)] = block[...]
    pair = ROWS // NOFF
    for o in range(NOFF):
        offset = offsets_ref[o]
        for member in range(out_ref.shape[0]):
            part = nearby[pl.ds(offset + pair * member, pair)]
            out_ref[member, pl.ds(pair * o, pair)] = part


def gather(blocks, offsets, members):
    rows = blocks[0].shape[0]
    vmem = pl.BlockSpec(memory_space=pltpu.VMEM)
    return pl.pallas_call(
        gather_kernel,
        out_shape=jax.ShapeDtypeStruct((members, ROWS, PHASES, LANES), jnp.bfloat16),
        in_specs=[pl.BlockSpec(memory_space=pltpu.SMEM)] + [vmem] * len(blocks),
        out_specs=vmem,
        scratch_shapes=[pltpu.VMEM((len(blocks) * rows, PHASES, LANES), jnp.bfloat16)],
        compiler_params=pltpu.CompilerParams(vmem_limit_bytes=16 * 1024 * 1024),
    )(offsets, *[blocks[index] for index in ORDER])


def ahead_on(array, axis, by):
    size = lax.axis_size(axis)
    return lax.ppermute(array, axis, [((i + by) % size, i) for i in range(size)])


def body(records, dead_flags, starts, offsets):
    rows = records.shape[0]
    dealt = deal(records, dead_flags)
    reach = lax.axis_size("loop") // 2
    blocks = [dealt] + [ahead_on(dealt, "loop", by) for by in range(1, reach + 1)]
    outgoing = gather(blocks, offsets, lax.axis_size("chan"))
    parts = lax.all_to_all(outgoing, "chan", split_axis=0, concat_axis=0, tiled=True)
    return stack(parts, starts)


def solution(mesh):
    in_specs = (P("loop", "chan"), P("loop"), P(), P())
    out_specs = P(("loop", "chan"), None, None)
    return jax.shard_map(body, mesh=mesh, in_specs=in_specs, out_specs=out_specs, check_vma=False)
```
